32 devices in a mesh: row: 8 (over z, y), col: 4 (over x, core).
Axes of the slice: x: 2, y: 2, z: 4, core: 2. Of those that a mesh axis runs over, the one named last changes fastest.
Arguments:
- rep_a: bfloat16 [4096, 512], P(('row', 'col')), may hold values from -100 to 100
- val_a: bfloat16 [4096, 512], P(('row', 'col')), may hold values from -6 to 6
- rep_b: bfloat16 [4096, 512], P(('row', 'col')), may hold values from -18 to 18
- val_b: bfloat16 [4096, 512], P(('row', 'col')), may hold values from -6 to 6
Outputs:
- mixed_a: float32 [4096, 512], P(('row', 'col'))
- mixed_b: float32 [4096, 512], P(('row', 'col'))
The draws below stay inside these ranges and needn't reach their ends.
All inputs are finite; a program needn't handle non-finite values.
Results may differ from the reference program's by a relative error of at most 0.0015.
Values may be sent and summed in bfloat16 or wider, within the bound.
A program may use at most 64 MiB of HBM per device.

```python
import math
import jax
import jax.numpy as jnp
from jax import lax

HEADS = 4
HEAD = 128
D = 512
NA = 4096
NB = 4096


def paired_sets(key):
    base = jax.random.fold_in(key, 7001)
    key_first, key_second = jax.random.split(base, 2)
    first_set = jnp.clip(jax.random.normal(key_first, (NA, D), jnp.float32), -6.0, 6.0)
    second_set = 2.8 * jnp.clip(jax.random.normal(key_second, (NB, D), jnp.float32), -6.0, 6.0)
    return (first_set, second_set)


def draw_rep_a(key, part):
    return paired_sets(key)[0].astype(jnp.bfloat16)


def draw_rep_b(key, part):
    return paired_sets(key)[1].astype(jnp.bfloat16)


def steps_of(own_key, dims, cuts, low, largest):
    def one(position, blocks):
        draws = jax.random.uniform(jax.random.fold_in(jax.random.fold_in(own_key, 6), position), (blocks,), jnp.float32, low / len(cuts), largest / len(cuts))
        return jnp.repeat(jnp.exp(draws), dims[position] // blocks).reshape((-1,) + (1,) * (len(dims) - position - 1))

    loudness = one(*cuts[0])
    for cut in cuts[1:]:
        loudness = loudness * one(*cut)
    return loudness


def scatter_about(key, dims, scale, bound, cuts=(), held_as=jnp.bfloat16):
    drawn = jax.random.normal(key, dims, jnp.float32) * scale
    if len(cuts) > 0:
        drawn = steps_of(key, dims, cuts, -0.22, 0.18) * drawn
    return jnp.clip(drawn, min=-bound, max=bound).astype(held_as)


def setup_inputs(seed: int = 0) -> dict:
    keys = jax.random.split(jax.random.key(seed), 5)
    return {
        "rep_a": draw_rep_a(jax.random.fold_in(keys[4], 71), 0),
        "val_a": scatter_about(keys[1], (NA, D), 1.0, 6.0, ((0, 32),)),
        "rep_b": draw_rep_b(jax.random.fold_in(keys[4], 71), 0),
        "val_b": scatter_about(keys[3], (NB, D), 1.0, 6.0, ((0, 32),)),
    }


def attend(queries, key_rows, value_rows):
    count = queries.shape[0]
    span_rows = math.gcd(512, count)
    inv_root = HEAD ** -0.5

    def one_block(query_block):
        pieces = []
        for head in range(HEADS):
            lower = head * HEAD
            logits = jnp.dot(query_block[:, lower:lower + HEAD], key_rows[:, lower:lower + HEAD].T, preferred_element_type=jnp.float32) * inv_root
            row_peak = jnp.max(logits, axis=1)
            weights = jnp.exp(logits - row_peak[:, None])
            totals = jnp.sum(weights, axis=1)
            numerator = jnp.dot(weights.astype(jnp.bfloat16), value_rows[:, lower:lower + HEAD], preferred_element_type=jnp.float32)
            pieces.append(numerator / totals[:, None])
        return jnp.concatenate(pieces, axis=1)

    grouped = queries.reshape(count // span_rows, span_rows, queries.shape[1])
    return lax.map(one_block, grouped).reshape(count, HEADS * HEAD)


def reference(rep_a, val_a, rep_b, val_b):
    return attend(rep_a, rep_b, val_b), attend(rep_b, rep_a, val_a)
```

```python
import functools

import jax
import jax.numpy as jnp
from jax import lax
from jax.experimental import pallas as pl
from jax.experimental.pallas import tpu as pltpu
from jax.sharding import PartitionSpec as P

HEADS = 4
HEAD = 128
STATS = 8
MESH = pl.DeviceIdType.MESH


def kernel(
    rows, cols,
    rep_a, val_a, rep_b, val_b, out_a, out_b,
    cut_a, cut_b, in_a, in_b, scores, peak_b,
    part_a, got_a, part_b, mate_b, got_b, done_a, done_b,
    cut_a_send, cut_b_send, a_recv, b_recv, a_send, b_send, mate_send,
    part_a_send, got_a_recv, mate_b_send, mate_b_recv, part_b_send, got_b_recv,
    done_a_send, done_b_send, done_a_recv, done_b_recv,
):
    Q, K = rows // HEADS, cols // 2
    n_a, n_b = rep_a.shape[0], rep_b.shape[0]
    row, col = lax.axis_index("row"), lax.axis_index("col")
    p, q = row // Q, row % Q
    k, c = col // 2, col % 2
    s = q * 2 + c
    inv_root = HEAD ** -0.5

    def head_at(d):
        return (p + d) % HEADS

    def at_head(d):
        return (head_at(d) * Q + q, col)

    def at_k(d):
        return (row, (k + d) % K * 2 + c)

    def at_q(d):
        return (p * Q + (q + d) % Q, col)

    mate = (row, k * 2 + 1 - c)

    def remote(src, dst, send, recv, device):
        return pltpu.make_async_remote_copy(
            src_ref=src, dst_ref=dst, send_sem=send, recv_sem=recv,
            device_id=device, device_id_type=MESH,
        )

    barrier = pltpu.get_barrier_semaphore()
    peers = [at_head(d) for d in range(1, HEADS)] + [at_k(d) for d in range(1, K)]
    peers += [at_q(d) for d in range(1, Q)] + [mate]
    for peer in peers:
        pl.semaphore_signal(barrier, inc=1, device_id=peer, device_id_type=MESH)

    for h in range(HEADS):
        lanes = slice(h * HEAD, (h + 1) * HEAD)
        cut_b[h, 0] = rep_b[:, lanes]
        cut_b[h, 1] = val_b[:, lanes]
        cut_a[h, 0] = rep_a[:, lanes]
        cut_a[h, 1] = val_a[:, lanes]
    in_b[s, p] = cut_b[p]
    in_a[k, p] = cut_a[p]
    peak_b[...] = jnp.full_like(peak_b, -jnp.inf)
    pl.semaphore_wait(barrier, len(peers))

    def cut_b_copy(d):
        h = head_at(d)
        return remote(cut_b.at[h], in_b.at[s, p], cut_b_send.at[d], b_recv.at[s, p], at_head(d))

    def cut_a_copy(d):
        h = head_at(d)
        return remote(cut_a.at[h], in_a.at[k, p], cut_a_send.at[d], a_recv.at[k, p], at_head(d))

    def a_copy(d, e):
        piece = in_a.at[k, head_at(e)]
        return remote(piece, piece, a_send.at[d, e], a_recv.at[k, head_at(e)], at_k(d))

    def b_copy(d, e):
        piece = in_b.at[s, head_at(e)]
        return remote(piece, piece, b_send.at[d, e], b_recv.at[s, head_at(e)], at_q(d))

    def mate_copy(d, e):
        r = (q + d) % Q * 2 + c
        piece = in_b.at[r, head_at(e)]
        return remote(piece, piece, mate_send.at[d, e], b_recv.at[r, head_at(e)], mate)

    def wait_b(r, e, device):
        piece = in_b.at[r, head_at(e)]
        remote(piece, piece, mate_send.at[0, 0], b_recv.at[r, head_at(e)], device).wait_recv()

    def wait_a(r, e, device):
        piece = in_a.at[r, head_at(e)]
        remote(piece, piece, mate_send.at[0, 0], a_recv.at[r, head_at(e)], device).wait_recv()

    for d in range(1, HEADS):
        cut_b_copy(d).start()
    for d in range(1, HEADS):
        cut_a_copy(d).start()
    for e in range(HEADS):
        if e:
            wait_b(s, e, at_head(e))
        for d in range(1, Q):
            b_copy(d, e).start()
        mate_copy(0, e).start()
        if e == 0:
            for d in range(1, K):
                a_copy(d, 0).start()
    for e in range(HEADS):
        for d in range(1, Q):
            wait_b((q + d) % Q * 2 + c, e, at_q(d))
            mate_copy(d, e).start()
    for e in range(HEADS):
        for d in range(Q):
            wait_b((q + d) % Q * 2 + 1 - c, e, mate)

    width = HEADS * n_b
    high = HEADS * n_a

    def row_block(kk, pp):
        start = pl.multiple_of((kk * HEADS + pp) * n_a, n_a)
        queries = in_a[kk, pp, 0]
        peak = jnp.full((n_a, 1), -jnp.inf, jnp.float32)
        for r in range(2 * Q):
            keys = in_b[r, :, 0].reshape(width, HEAD)
            logits = lax.dot_general(
                queries, keys, (((1,), (1,)), ((), ())), preferred_element_type=jnp.float32
            ) * inv_root
            scores[r, pl.ds(start, n_a), :] = logits
            peak_b[r] = jnp.maximum(peak_b[r], jnp.max(logits, axis=0, keepdims=True))
            peak = jnp.maximum(peak, jnp.max(logits, axis=1, keepdims=True))
        total = jnp.zeros((n_a, 1), jnp.float32)
        num = jnp.zeros((n_a, HEAD), jnp.float32)
        for r in range(2 * Q):
            values = in_b[r, :, 1].reshape(width, HEAD)
            weights = jnp.exp(scores[r, pl.ds(start, n_a), :] - peak)
            total += jnp.sum(weights, axis=1, keepdims=True)
            num += jnp.dot(
                weights.astype(jnp.bfloat16), values, preferred_element_type=jnp.float32
            )
        lane = lax.broadcasted_iota(jnp.int32, (n_a, HEAD), 1)
        stats = jnp.where(lane == 0, peak, total)
        part_a[kk, pp, 0:HEAD] = num.T
        part_a[kk, pp, HEAD:HEAD + STATS] = stats.T[0:STATS]

    def part_a_copy(d, e):
        there = (k + d) % K
        h = head_at(e)
        return remote(
            part_a.at[there, h], got_a.at[k, h], part_a_send.at[d, e], got_a_recv.at[k, h], at_k(d)
        )

    def other_rows(e):
        for d in range(1, K):
            kk = (k + d) % K
            wait_a(kk, e, at_k(d))
            row_block(kk, head_at(e))
            part_a_copy(d, e).start()

    row_block(k, p)

    @pl.loop(1, HEADS)
    def _(e):
        wait_a(k, e, at_head(e))
        for d in range(1, K):
            a_copy(d, e).start()
        row_block(k, head_at(e))
        other_rows(e - 1)

    other_rows(HEADS - 1)

    values_t = in_a[:, :, 1].reshape(K * high, HEAD).T

    def col_block(r):
        peak = peak_b[r]
        weights = jnp.exp(scores[r] - peak)
        total = jnp.sum(weights, axis=0, keepdims=True)
        num = jnp.dot(values_t, weights.astype(jnp.bfloat16), preferred_element_type=jnp.float32)
        sub = lax.broadcasted_iota(jnp.int32, (STATS, width), 0)
        stats = jnp.where(sub == 0, peak, total)
        for h in range(HEADS):
            part_b[r, h, 0:HEAD] = num[:, h * n_b:(h + 1) * n_b]
            part_b[r, h, HEAD:HEAD + STATS] = stats[:, h * n_b:(h + 1) * n_b]

    def mate_b_copy(d):
        qq = (q + d) % Q
        return remote(
            part_b.at[qq * 2 + 1 - c], mate_b.at[qq], mate_b_send.at[d], mate_b_recv.at[qq], mate
        )

    def part_b_copy(d, e):
        there = (q + d) % Q * 2 + c
        h = head_at(e)
        return remote(
            part_b.at[there, h], got_b.at[q, h], part_b_send.at[d, e], got_b_recv.at[q, h], at_q(d)
        )

    order = [d % Q for d in range(1, Q + 1)]
    for d in order:
        col_block((q + d) % Q * 2 + 1 - c)
        mate_b_copy(d).start()
    for d in order:
        col_block((q + d) % Q * 2 + c)

    def merged(parts):
        peak = functools.reduce(jnp.maximum, [x[HEAD:HEAD + 1] for x in parts])
        scales = [jnp.exp(x[HEAD:HEAD + 1] - peak) for x in parts]
        num = sum(x[0:HEAD] * w for x, w in zip(parts, scales))
        total = sum(x[HEAD + 1:HEAD + 2] * w for x, w in zip(parts, scales))
        return num, total, peak

    for d in order:
        qq = (q + d) % Q
        mate_b_copy(d).wait_recv()
        for e in range(HEADS):
            h = head_at(e)
            num, total, peak = merged([part_b[qq * 2 + c, h], mate_b[qq, h]])
            part_b[qq * 2 + c, h, 0:HEAD] = num
            part_b[qq * 2 + c, h, HEAD:HEAD + 1] = peak
            part_b[qq * 2 + c, h, HEAD + 1:HEAD + 2] = total
            if d:
                part_b_copy(d, e).start()

    own_lanes = pl.ds(pl.multiple_of(p * HEAD, HEAD), HEAD)

    def done_copy(e, done, out, send, recv):
        return remote(done.at[head_at(e)], out.at[:, own_lanes], send.at[e], recv.at[p], at_head(e))

    def wait_done(e, done, out, send, recv):
        lanes = pl.ds(pl.multiple_of(head_at(e) * HEAD, HEAD), HEAD)
        remote(
            done.at[head_at(e)], out.at[:, lanes], send.at[e], recv.at[head_at(e)], at_head(e)
        ).wait_recv()

    def finish(e, parts, done, out, send, recv):
        num, total, _ = merged(parts)
        result = (num / total).T
        if e:
            done[head_at(e)] = result
            done_copy(e, done, out, send, recv).start()
        else:
            out[:, own_lanes] = result

    last = [d % HEADS for d in range(1, HEADS + 1)]
    for e in last:
        h = head_at(e)
        parts = [part_a[k, h]]
        for d in range(1, K):
            kk = (k + d) % K
            remote(
                part_a.at[kk, h], got_a.at[kk, h], part_a_send.at[d, e], got_a_recv.at[kk, h],
                at_k(d),
            ).wait_recv()
            parts.append(got_a[kk, h])
        finish(e, parts, done_a, out_a, done_a_send, done_a_recv)
    for e in last:
        h = head_at(e)
        parts = [part_b[s, h]]
        for d in range(1, Q):
            qq = (q + d) % Q
            remote(
                part_b.at[qq * 2 + c, h], got_b.at[qq, h], part_b_send.at[d, e],
                got_b_recv.at[qq, h], at_q(d),
            ).wait_recv()
            parts.append(got_b[qq, h])
        finish(e, parts, done_b, out_b, done_b_send, done_b_recv)

    for d in range(1, HEADS):
        cut_b_copy(d).wait_send()
        cut_a_copy(d).wait_send()
    for e in range(HEADS):
        for d in range(1, K):
            a_copy(d, e).wait_send()
            part_a_copy(d, e).wait_send()
        for d in range(Q):
            if d:
                b_copy(d, e).wait_send()
                part_b_copy(d, e).wait_send()
            mate_copy(d, e).wait_send()
    for d in range(Q):
        mate_b_copy(d).wait_send()
    for e in range(1, HEADS):
        done_copy(e, done_a, out_a, done_a_send, done_a_recv).wait_send()
        done_copy(e, done_b, out_b, done_b_send, done_b_recv).wait_send()
    for e in range(1, HEADS):
        wait_done(e, done_a, out_a, done_a_send, done_a_recv)
        wait_done(e, done_b, out_b, done_b_send, done_b_recv)


def on_device(rows, cols, rep_a, val_a, rep_b, val_b):
    Q, K = rows // HEADS, cols // 2
    n_a, n_b = rep_a.shape[0], rep_b.shape[0]
    f32, bf16 = jnp.float32, jnp.bfloat16
    tall = HEAD + STATS
    dma = pltpu.SemaphoreType.DMA
    vmem = pl.BlockSpec(memory_space=pltpu.VMEM)
    tile = K * HEADS * n_a * 2 * Q * HEADS * n_b
    return pl.pallas_call(
        functools.partial(kernel, rows, cols),
        out_shape=(
            jax.ShapeDtypeStruct(rep_a.shape, f32),
            jax.ShapeDtypeStruct(rep_b.shape, f32),
        ),
        in_specs=[vmem] * 4,
        out_specs=(vmem, vmem),
        scratch_shapes=[
            pltpu.VMEM((HEADS, 2, n_a, HEAD), bf16),
            pltpu.VMEM((HEADS, 2, n_b, HEAD), bf16),
            pltpu.VMEM((K, HEADS, 2, n_a, HEAD), bf16),
            pltpu.VMEM((2 * Q, HEADS, 2, n_b, HEAD), bf16),
            pltpu.VMEM((2 * Q, K * HEADS * n_a, HEADS * n_b), f32),
            pltpu.VMEM((2 * Q, 1, HEADS * n_b), f32),
            pltpu.VMEM((K, HEADS, tall, n_a), f32),
            pltpu.VMEM((K, HEADS, tall, n_a), f32),
            pltpu.VMEM((2 * Q, HEADS, tall, n_b), f32),
            pltpu.VMEM((Q, HEADS, tall, n_b), f32),
            pltpu.VMEM((Q, HEADS, tall, n_b), f32),
            pltpu.VMEM((HEADS, n_a, HEAD), f32),
            pltpu.VMEM((HEADS, n_b, HEAD), f32),
            dma((HEADS,)), dma((HEADS,)),
            dma((K, HEADS)), dma((2 * Q, HEADS)),
            dma((K, HEADS)), dma((Q, HEADS)), dma((Q, HEADS)),
            dma((K, HEADS)), dma((K, HEADS)),
            dma((Q,)), dma((Q,)),
            dma((Q, HEADS)), dma((Q, HEADS)),
            dma((HEADS,)), dma((HEADS,)), dma((HEADS,)), dma((HEADS,)),
        ],
        compiler_params=pltpu.CompilerParams(
            collective_id=0, has_side_effects=True, vmem_limit_bytes=48 * 1024 * 1024
        ),
        cost_estimate=pl.CostEstimate(
            flops=6 * tile * HEAD, bytes_accessed=6 * 1024 * (n_a + n_b), transcendentals=2 * tile
        ),
    )(rep_a, val_a, rep_b, val_b)


def solution(mesh):
    rows, cols = mesh.shape["row"], mesh.shape["col"]
    placed = P(("row", "col"), None)
    return jax.shard_map(
        functools.partial(on_device, rows, cols),
        mesh=mesh,
        in_specs=(placed,) * 4,
        out_specs=(placed, placed),
        check_vma=False,
    )
```

```python
import functools
import math

import jax
import jax.numpy as jnp
from jax import lax
from jax.experimental import pallas as pl
from jax.experimental.pallas import tpu as pltpu
from jax.sharding import PartitionSpec as P

HEADS = 4
HEAD = 128
STATS = 8
MESH = pl.DeviceIdType.MESH


def kernel(
    rows, cols,
    rep_a, val_a, rep_b, val_b, out_a, out_b,
    in_a, in_b, keys_t, scores, peak_b,
    part_a, got_a, part_b, mate_b, got_b, done_a, done_b,
    own, cut_a_send, cut_b_send, a_recv, b_recv, a_send, b_send, mate_send,
    part_a_send, got_a_recv, mate_b_send, mate_b_recv, part_b_send, got_b_recv,
    done_a_send, done_b_send, done_a_recv, done_b_recv,
):
    Q, K = rows // HEADS, cols // 2
    n_a, n_b = rep_a.shape[0], rep_b.shape[0]
    row, col = lax.axis_index("row"), lax.axis_index("col")
    p, q = row // Q, row % Q
    k, c = col // 2, col % 2
    s = q * 2 + c
    to_log2 = HEAD ** -0.5 * math.log2(math.e)

    def head_at(d):
        return (p + d) % HEADS

    def at_head(d):
        return (head_at(d) * Q + q, col)

    def at_k(d):
        return (row, (k + d) % K * 2 + c)

    def at_q(d):
        return (p * Q + (q + d) % Q, col)

    mate = (row, k * 2 + 1 - c)

    def remote(src, dst, send, recv, device):
        return pltpu.make_async_remote_copy(
            src_ref=src, dst_ref=dst, send_sem=send, recv_sem=recv,
            device_id=device, device_id_type=MESH,
        )

    barrier = pltpu.get_barrier_semaphore()
    peers = [at_head(d) for d in range(1, HEADS)] + [at_k(d) for d in range(1, K)]
    peers += [at_q(d) for d in range(1, Q)] + [mate]
    for peer in peers:
        pl.semaphore_signal(barrier, inc=1, device_id=peer, device_id_type=MESH)

    def head_lanes(h):
        return pl.ds(pl.multiple_of(h * HEAD, HEAD), HEAD)

    own_lanes = head_lanes(p)
    own_copies = [
        pltpu.make_async_copy(x.at[:, own_lanes], y, own.at[i])
        for i, (x, y) in enumerate([
            (rep_b, in_b.at[s, p, 0]), (val_b, in_b.at[s, p, 1]),
            (rep_a, in_a.at[p, k, 0]), (val_a, in_a.at[p, k, 1]),
        ])
    ]
    for copy in own_copies:
        copy.start()
    peak_b[...] = jnp.full_like(peak_b, -jnp.inf)
    pl.semaphore_wait(barrier, len(peers))

    def cut_b_copy(d, i):
        return remote(
            (rep_b, val_b)[i].at[:, head_lanes(head_at(d))], in_b.at[s, p, i],
            cut_b_send.at[d, i], b_recv.at[s, p], at_head(d),
        )

    def cut_a_copy(d, i):
        return remote(
            (rep_a, val_a)[i].at[:, head_lanes(head_at(d))], in_a.at[p, k, i],
            cut_a_send.at[d, i], a_recv.at[k, p], at_head(d),
        )

    def a_copy(d, e):
        piece = in_a.at[head_at(e), k]
        return remote(piece, piece, a_send.at[d, e], a_recv.at[k, head_at(e)], at_k(d))

    def b_copy(d, e):
        piece = in_b.at[s, head_at(e)]
        return remote(piece, piece, b_send.at[d, e], b_recv.at[s, head_at(e)], at_q(d))

    def mate_copy(d, e):
        r = (q + d) % Q * 2 + c
        piece = in_b.at[r, head_at(e)]
        return remote(piece, piece, mate_send.at[d, e], b_recv.at[r, head_at(e)], mate)

    def wait_b(r, e, device):
        piece = in_b.at[r, head_at(e)]
        remote(piece, piece, mate_send.at[0, 0], b_recv.at[r, head_at(e)], device).wait_recv()

    def wait_a(r, e, device):
        piece = in_a.at[head_at(e), r]
        remote(piece, piece, mate_send.at[0, 0], a_recv.at[r, head_at(e)], device).wait_recv()

    for cut in (cut_b_copy, cut_a_copy):
        for d in range(1, HEADS):
            for i in range(2):
                cut(d, i).start()
    for copy in own_copies:
        copy.wait()
    for e in range(HEADS):
        if e:
            wait_b(s, e, at_head(e))
        for d in range(1, Q):
            b_copy(d, e).start()
        mate_copy(0, e).start()
        if e == 0:
            for d in range(1, K):
                a_copy(d, 0).start()
    for e in range(HEADS):
        for d in range(1, Q):
            wait_b((q + d) % Q * 2 + c, e, at_q(d))
            mate_copy(d, e).start()
    for e in range(HEADS):
        for d in range(Q):
            wait_b((q + d) % Q * 2 + 1 - c, e, mate)
    for r in range(2 * Q):
        keys_t[r] = in_b[r, :, 0].reshape(HEADS * n_b, HEAD).T

    width = HEADS * n_b
    span = K * n_a

    def row_block(pp):
        start = pl.multiple_of(pp * span, span)
        queries = in_a[pp, :, 0].reshape(span, HEAD)
        peak = jnp.full((span, 1), -jnp.inf, jnp.float32)
        for r in range(2 * Q):
            logits = jnp.dot(queries, keys_t[r], preferred_element_type=jnp.float32) * to_log2
            scores[r, pl.ds(start, span), :] = logits
            peak_b[r] = jnp.maximum(peak_b[r], jnp.max(logits, axis=0, keepdims=True))
            peak = jnp.maximum(peak, jnp.max(logits, axis=1, keepdims=True))
        total = jnp.zeros((span, 1), jnp.float32)
        num = jnp.zeros((span, HEAD), jnp.float32)
        for r in range(2 * Q):
            values = in_b[r, :, 1].reshape(width, HEAD)
            weights = jnp.exp2(scores[r, pl.ds(start, span), :] - peak)
            total += jnp.sum(weights, axis=1, keepdims=True)
            num += jnp.dot(
                weights.astype(jnp.bfloat16), values, preferred_element_type=jnp.float32
            )
        lane = lax.broadcasted_iota(jnp.int32, (span, HEAD), 1)
        stats = jnp.where(lane == 0, peak, total)
        for kk in range(K):
            mine = slice(kk * n_a, (kk + 1) * n_a)
            part_a[kk, pp, 0:HEAD] = num[mine].T
            part_a[kk, pp, HEAD:HEAD + STATS] = stats[mine].T[0:STATS]

    def part_a_copy(d, e):
        there = (k + d) % K
        h = head_at(e)
        return remote(
            part_a.at[there, h], got_a.at[k, h], part_a_send.at[d, e], got_a_recv.at[k, h], at_k(d)
        )

    def rows_of(e):
        for d in range(1, K):
            wait_a((k + d) % K, e, at_k(d))
        row_block(head_at(e))
        for d in range(1, K):
            part_a_copy(d, e).start()

    @pl.loop(0, HEADS - 1)
    def _(e):
        wait_a(k, e + 1, at_head(e + 1))
        for d in range(1, K):
            a_copy(d, e + 1).start()
        rows_of(e)

    rows_of(HEADS - 1)

    values_t = in_a[:, :, 1].reshape(HEADS * span, HEAD).T

    def col_block(r):
        peak = peak_b[r]
        weights = jnp.exp2(scores[r] - peak)
        total = jnp.sum(weights, axis=0, keepdims=True)
        num = jnp.dot(values_t, weights.astype(jnp.bfloat16), preferred_element_type=jnp.float32)
        sub = lax.broadcasted_iota(jnp.int32, (STATS, width), 0)
        stats = jnp.where(sub == 0, peak, total)
        for h in range(HEADS):
            part_b[r, h, 0:HEAD] = num[:, h * n_b:(h + 1) * n_b]
            part_b[r, h, HEAD:HEAD + STATS] = stats[:, h * n_b:(h + 1) * n_b]

    def mate_b_copy(d):
        qq = (q + d) % Q
        return remote(
            part_b.at[qq * 2 + 1 - c], mate_b.at[qq], mate_b_send.at[d], mate_b_recv.at[qq], mate
        )

    def part_b_copy(d, e):
        there = (q + d) % Q * 2 + c
        h = head_at(e)
        return remote(
            part_b.at[there, h], got_b.at[q, h], part_b_send.at[d, e], got_b_recv.at[q, h], at_q(d)
        )

    order = [d % Q for d in range(1, Q + 1)]

    def merged(parts):
        peak = functools.reduce(jnp.maximum, [x[HEAD:HEAD + 1] for x in parts])
        scales = [jnp.exp2(x[HEAD:HEAD + 1] - peak) for x in parts]
        num = sum(x[0:HEAD] * w for x, w in zip(parts, scales))
        total = sum(x[HEAD + 1:HEAD + 2] * w for x, w in zip(parts, scales))
        return num, total, peak

    def done_copy(e, done, out, send, recv):
        return remote(done.at[head_at(e)], out.at[:, own_lanes], send.at[e], recv.at[p], at_head(e))

    def wait_done(e, done, out, send, recv):
        remote(
            done.at[head_at(e)], out.at[:, head_lanes(head_at(e))], send.at[e], recv.at[head_at(e)], at_head(e)
        ).wait_recv()

    def finish(e, parts, done, out, send, recv):
        num, total, _ = merged(parts)
        result = (num / total).T
        if e:
            done[head_at(e)] = result
            done_copy(e, done, out, send, recv).start()
        else:
            out[:, own_lanes] = result

    last = [d % HEADS for d in range(1, HEADS + 1)]

    def finish_a(e):
        h = head_at(e)
        parts = [part_a[k, h]]
        for d in range(1, K):
            kk = (k + d) % K
            remote(
                part_a.at[kk, h], got_a.at[kk, h], part_a_send.at[d, e], got_a_recv.at[kk, h],
                at_k(d),
            ).wait_recv()
            parts.append(got_a[kk, h])
        finish(e, parts, done_a, out_a, done_a_send, done_a_recv)

    blocks = 2 * Q
    for i in range(blocks):
        d = order[i % Q]
        if i < Q:
            col_block((q + d) % Q * 2 + 1 - c)
            mate_b_copy(d).start()
        else:
            col_block((q + d) % Q * 2 + c)
        for e in last[i * HEADS // blocks:(i + 1) * HEADS // blocks]:
            finish_a(e)

    for d in order:
        qq = (q + d) % Q
        mate_b_copy(d).wait_recv()
        for e in range(HEADS):
            h = head_at(e)
            num, total, peak = merged([part_b[qq * 2 + c, h], mate_b[qq, h]])
            part_b[qq * 2 + c, h, 0:HEAD] = num
            part_b[qq * 2 + c, h, HEAD:HEAD + 1] = peak
            part_b[qq * 2 + c, h, HEAD + 1:HEAD + 2] = total
            if d:
                part_b_copy(d, e).start()

    for e in last:
        h = head_at(e)
        parts = [part_b[s, h]]
        for d in range(1, Q):
            qq = (q + d) % Q
            remote(
                part_b.at[qq * 2 + c, h], got_b.at[qq, h], part_b_send.at[d, e],
                got_b_recv.at[qq, h], at_q(d),
            ).wait_recv()
            parts.append(got_b[qq, h])
        finish(e, parts, done_b, out_b, done_b_send, done_b_recv)

    for d in range(1, HEADS):
        for i in range(2):
            cut_b_copy(d, i).wait_send()
            cut_a_copy(d, i).wait_send()
    for e in range(HEADS):
        for d in range(1, K):
            a_copy(d, e).wait_send()
            part_a_copy(d, e).wait_send()
        for d in range(Q):
            if d:
                b_copy(d, e).wait_send()
                part_b_copy(d, e).wait_send()
            mate_copy(d, e).wait_send()
    for d in range(Q):
        mate_b_copy(d).wait_send()
    for e in range(1, HEADS):
        done_copy(e, done_a, out_a, done_a_send, done_a_recv).wait_send()
        done_copy(e, done_b, out_b, done_b_send, done_b_recv).wait_send()
    for e in range(1, HEADS):
        wait_done(e, done_a, out_a, done_a_send, done_a_recv)
        wait_done(e, done_b, out_b, done_b_send, done_b_recv)


def on_device(rows, cols, rep_a, val_a, rep_b, val_b):
    Q, K = rows // HEADS, cols // 2
    n_a, n_b = rep_a.shape[0], rep_b.shape[0]
    f32, bf16 = jnp.float32, jnp.bfloat16
    tall = HEAD + STATS
    dma = pltpu.SemaphoreType.DMA
    vmem = pl.BlockSpec(memory_space=pltpu.VMEM)
    hbm = pl.BlockSpec(memory_space=pltpu.HBM)
    tile = K * HEADS * n_a * 2 * Q * HEADS * n_b
    return pl.pallas_call(
        functools.partial(kernel, rows, cols),
        out_shape=(
            jax.ShapeDtypeStruct(rep_a.shape, f32),
            jax.ShapeDtypeStruct(rep_b.shape, f32),
        ),
        in_specs=[hbm] * 4,
        out_specs=(vmem, vmem),
        scratch_shapes=[
            pltpu.VMEM((HEADS, K, 2, n_a, HEAD), bf16),
            pltpu.VMEM((2 * Q, HEADS, 2, n_b, HEAD), bf16),
            pltpu.VMEM((2 * Q, HEAD, HEADS * n_b), bf16),
            pltpu.VMEM((2 * Q, K * HEADS * n_a, HEADS * n_b), f32),
            pltpu.VMEM((2 * Q, 1, HEADS * n_b), f32),
            pltpu.VMEM((K, HEADS, tall, n_a), f32),
            pltpu.VMEM((K, HEADS, tall, n_a), f32),
            pltpu.VMEM((2 * Q, HEADS, tall, n_b), f32),
            pltpu.VMEM((Q, HEADS, tall, n_b), f32),
            pltpu.VMEM((Q, HEADS, tall, n_b), f32),
            pltpu.VMEM((HEADS, n_a, HEAD), f32),
            pltpu.VMEM((HEADS, n_b, HEAD), f32),
            dma((4,)), dma((HEADS, 2)), dma((HEADS, 2)),
            dma((K, HEADS)), dma((2 * Q, HEADS)),
            dma((K, HEADS)), dma((Q, HEADS)), dma((Q, HEADS)),
            dma((K, HEADS)), dma((K, HEADS)),
            dma((Q,)), dma((Q,)),
            dma((Q, HEADS)), dma((Q, HEADS)),
            dma((HEADS,)), dma((HEADS,)), dma((HEADS,)), dma((HEADS,)),
        ],
        compiler_params=pltpu.CompilerParams(
            collective_id=0, has_side_effects=True, vmem_limit_bytes=48 * 1024 * 1024
        ),
        cost_estimate=pl.CostEstimate(
            flops=6 * tile * HEAD, bytes_accessed=6 * 1024 * (n_a + n_b), transcendentals=2 * tile
        ),
    )(rep_a, val_a, rep_b, val_b)


def solution(mesh):
    rows, cols = mesh.shape["row"], mesh.shape["col"]
    placed = P(("row", "col"), None)
    return jax.shard_map(
        functools.partial(on_device, rows, cols),
        mesh=mesh,
        in_specs=(placed,) * 4,
        out_specs=(placed, placed),
        check_vma=False,
    )
```

```python
import functools
import math

import jax
import jax.numpy as jnp
from jax import lax
from jax.experimental import pallas as pl
from jax.experimental.pallas import tpu as pltpu
from jax.sharding import PartitionSpec as P

HEADS = 4
HEAD = 128
STATS = 8
EXTRA = 16
BINADES = 248.0
MESH = pl.DeviceIdType.MESH


def code_of(x, scale):
    code = jnp.exp2(jnp.abs(x) * (BINADES / scale) - BINADES / 2)
    return jnp.where(x < 0, -code, code).astype(jnp.bfloat16)


def value_of(code, scale):
    code = code.astype(jnp.float32)
    size = jnp.log(jnp.abs(code)) * (1 / (math.log(2) * BINADES)) + 0.5
    return jnp.where(code < 0, -size, size) * scale


def scale_of(x):
    largest = jnp.max(jnp.abs(x), axis=0, keepdims=True) * 1.01 + 1e-30
    return largest.astype(jnp.bfloat16)


def three_terms(x):
    terms = []
    for _ in range(3):
        term = x.astype(jnp.bfloat16).astype(jnp.float32)
        terms.append(term)
        x = x - term
    return terms


def packed_part(num, total, peak):
    mean = num / total
    scale = scale_of(mean).astype(jnp.float32)
    rows = [scale] + three_terms(peak) + three_terms(total)
    sub = lax.broadcasted_iota(jnp.int32, (EXTRA, num.shape[1]), 0)
    extra = jnp.zeros((EXTRA, num.shape[1]), jnp.float32)
    for i, x in enumerate(rows):
        extra = jnp.where(sub == i, x, extra)
    return code_of(mean, scale), extra.astype(jnp.bfloat16)


def unpacked_part(codes, extra):
    extra = extra.astype(jnp.float32)
    peak = extra[1:2] + extra[2:3] + extra[3:4]
    total = extra[4:5] + extra[5:6] + extra[6:7]
    return value_of(codes, extra[0:1]) * total, total, peak


def merged(parts):
    peak = functools.reduce(jnp.maximum, [x[2] for x in parts])
    scales = [jnp.exp2(x[2] - peak) for x in parts]
    num = sum(x[0] * w for x, w in zip(parts, scales))
    total = sum(x[1] * w for x, w in zip(parts, scales))
    return num, total, peak


def kernel(
    rows, cols,
    rep_a, val_a, rep_b, val_b, out_a, out_b,
    in_a, in_b, keys_t, scores, peak_b,
    part_a, code_a, got_a, part_b, mate_b, code_b, got_b, done_a, done_b, back_a, back_b,
    own, cut_a_send, cut_b_send, a_recv, b_recv, a_send, b_send, mate_send,
    part_a_send, got_a_recv, mate_b_send, mate_b_recv, part_b_send, got_b_recv,
    done_a_send, done_b_send, done_a_recv, done_b_recv,
):
    Q, K = rows // HEADS, cols // 2
    n_a, n_b = rep_a.shape[0], rep_b.shape[0]
    row, col = lax.axis_index("row"), lax.axis_index("col")
    p, q = row // Q, row % Q
    k, c = col // 2, col % 2
    s = q * 2 + c
    to_log2 = HEAD ** -0.5 * math.log2(math.e)

    def head_at(d):
        return (p + d) % HEADS

    def at_head(d):
        return (head_at(d) * Q + q, col)

    def at_k(d):
        return (row, (k + d) % K * 2 + c)

    def at_q(d):
        return (p * Q + (q + d) % Q, col)

    mate = (row, k * 2 + 1 - c)

    def remote(src, dst, send, recv, device):
        return pltpu.make_async_remote_copy(
            src_ref=src, dst_ref=dst, send_sem=send, recv_sem=recv,
            device_id=device, device_id_type=MESH,
        )

    barrier = pltpu.get_barrier_semaphore()
    peers = [at_head(d) for d in range(1, HEADS)] + [at_k(d) for d in range(1, K)]
    peers += [at_q(d) for d in range(1, Q)] + [mate]
    for peer in peers:
        pl.semaphore_signal(barrier, inc=1, device_id=peer, device_id_type=MESH)

    def head_lanes(h):
        return pl.ds(pl.multiple_of(h * HEAD, HEAD), HEAD)

    own_lanes = head_lanes(p)
    own_copies = [
        pltpu.make_async_copy(x.at[:, own_lanes], y, own.at[i])
        for i, (x, y) in enumerate([
            (rep_b, in_b.at[s, p, 0]), (val_b, in_b.at[s, p, 1]),
            (rep_a, in_a.at[p, k, 0]), (val_a, in_a.at[p, k, 1]),
        ])
    ]
    for copy in own_copies:
        copy.start()
    peak_b[...] = jnp.full_like(peak_b, -jnp.inf)
    pl.semaphore_wait(barrier, len(peers))

    def cut_b_copy(d, i):
        return remote(
            (rep_b, val_b)[i].at[:, head_lanes(head_at(d))], in_b.at[s, p, i],
            cut_b_send.at[d, i], b_recv.at[s, p], at_head(d),
        )

    def cut_a_copy(d, i):
        return remote(
            (rep_a, val_a)[i].at[:, head_lanes(head_at(d))], in_a.at[p, k, i],
            cut_a_send.at[d, i], a_recv.at[k, p], at_head(d),
        )

    def a_copy(d, e):
        piece = in_a.at[head_at(e), k]
        return remote(piece, piece, a_send.at[d, e], a_recv.at[k, head_at(e)], at_k(d))

    def b_copy(d, e):
        piece = in_b.at[s, head_at(e)]
        return remote(piece, piece, b_send.at[d, e], b_recv.at[s, head_at(e)], at_q(d))

    def mate_copy(d, e):
        r = (q + d) % Q * 2 + c
        piece = in_b.at[r, head_at(e)]
        return remote(piece, piece, mate_send.at[d, e], b_recv.at[r, head_at(e)], mate)

    def wait_b(r, e, device):
        piece = in_b.at[r, head_at(e)]
        remote(piece, piece, mate_send.at[0, 0], b_recv.at[r, head_at(e)], device).wait_recv()

    def wait_a(r, e, device):
        piece = in_a.at[head_at(e), r]
        remote(piece, piece, mate_send.at[0, 0], a_recv.at[r, head_at(e)], device).wait_recv()

    for cut in (cut_b_copy, cut_a_copy):
        for d in range(1, HEADS):
            for i in range(2):
                cut(d, i).start()
    for copy in own_copies:
        copy.wait()
    for e in range(HEADS):
        if e:
            wait_b(s, e, at_head(e))
        for d in range(1, Q):
            b_copy(d, e).start()
        mate_copy(0, e).start()
        if e == 0:
            for d in range(1, K):
                a_copy(d, 0).start()
    for e in range(HEADS):
        for d in range(1, Q):
            wait_b((q + d) % Q * 2 + c, e, at_q(d))
            mate_copy(d, e).start()
    for e in range(HEADS):
        for d in range(Q):
            wait_b((q + d) % Q * 2 + 1 - c, e, mate)
    for r in range(2 * Q):
        keys_t[r] = in_b[r, :, 0].reshape(HEADS * n_b, HEAD).T

    width = HEADS * n_b
    span = K * n_a

    def row_block(pp):
        start = pl.multiple_of(pp * span, span)
        queries = in_a[pp, :, 0].reshape(span, HEAD)
        peak = jnp.full((span, 1), -jnp.inf, jnp.float32)
        for r in range(2 * Q):
            logits = jnp.dot(queries, keys_t[r], preferred_element_type=jnp.float32) * to_log2
            scores[r, pl.ds(start, span), :] = logits
            peak_b[r] = jnp.maximum(peak_b[r], jnp.max(logits, axis=0, keepdims=True))
            peak = jnp.maximum(peak, jnp.max(logits, axis=1, keepdims=True))
        total = jnp.zeros((span, 1), jnp.float32)
        num = jnp.zeros((span, HEAD), jnp.float32)
        for r in range(2 * Q):
            values = in_b[r, :, 1].reshape(width, HEAD)
            weights = jnp.exp2(scores[r, pl.ds(start, span), :] - peak)
            total += jnp.sum(weights, axis=1, keepdims=True)
            num += jnp.dot(
                weights.astype(jnp.bfloat16), values, preferred_element_type=jnp.float32
            )
        lane = lax.broadcasted_iota(jnp.int32, (span, HEAD), 1)
        stats = jnp.where(lane == 0, peak, total)
        for kk in range(K):
            mine = slice(kk * n_a, (kk + 1) * n_a)
            num_t = num[mine].T
            stats_t = stats[mine].T[0:STATS]
            part_a[kk, pp, 0:HEAD] = num_t
            part_a[kk, pp, HEAD:HEAD + STATS] = stats_t
            codes, extra = packed_part(num_t, stats_t[1:2], stats_t[0:1])
            code_a[kk, pp, 0:HEAD] = codes
            code_a[kk, pp, HEAD:HEAD + EXTRA] = extra

    def part_a_copy(d, e):
        there = (k + d) % K
        h = head_at(e)
        return remote(
            code_a.at[there, h], got_a.at[k, h], part_a_send.at[d, e], got_a_recv.at[k, h], at_k(d)
        )

    def rows_of(e):
        for d in range(1, K):
            wait_a((k + d) % K, e, at_k(d))
        row_block(head_at(e))
        for d in range(1, K):
            part_a_copy(d, e).start()

    @pl.loop(0, HEADS - 1)
    def _(e):
        wait_a(k, e + 1, at_head(e + 1))
        for d in range(1, K):
            a_copy(d, e + 1).start()
        rows_of(e)

    rows_of(HEADS - 1)

    values_t = in_a[:, :, 1].reshape(HEADS * span, HEAD).T

    def col_block(r):
        peak = peak_b[r]
        weights = jnp.exp2(scores[r] - peak)
        total = jnp.sum(weights, axis=0, keepdims=True)
        num = jnp.dot(values_t, weights.astype(jnp.bfloat16), preferred_element_type=jnp.float32)
        sub = lax.broadcasted_iota(jnp.int32, (STATS, width), 0)
        stats = jnp.where(sub == 0, peak, total)
        for h in range(HEADS):
            part_b[r, h, 0:HEAD] = num[:, h * n_b:(h + 1) * n_b]
            part_b[r, h, HEAD:HEAD + STATS] = stats[:, h * n_b:(h + 1) * n_b]

    def mate_b_copy(d):
        qq = (q + d) % Q
        return remote(
            part_b.at[qq * 2 + 1 - c], mate_b.at[qq], mate_b_send.at[d], mate_b_recv.at[qq], mate
        )

    def part_b_copy(d, e):
        h = head_at(e)
        return remote(
            code_b.at[(q + d) % Q, h], got_b.at[q, h], part_b_send.at[d, e], got_b_recv.at[q, h], at_q(d)
        )

    order = [d % Q for d in range(1, Q + 1)]

    def part_of(ref):
        return ref[0:HEAD], ref[HEAD + 1:HEAD + 2], ref[HEAD:HEAD + 1]

    def sent_part_of(ref):
        return unpacked_part(ref[0:HEAD], ref[HEAD:HEAD + EXTRA])

    def done_copy(e, done, back, send, recv):
        return remote(done.at[head_at(e)], back.at[p], send.at[e], recv.at[p], at_head(e))

    def take_done(e, done, back, out, send, recv):
        h = head_at(e)
        remote(done.at[h], back.at[h], send.at[e], recv.at[h], at_head(e)).wait_recv()
        n = out.shape[0]
        scale = back[h, n:n + EXTRA].astype(jnp.float32)[0:1]
        out[:, head_lanes(h)] = value_of(back[h, 0:n], scale)

    def finish(e, parts, done, back, out, send, recv):
        num, total, _ = merged(parts)
        result = (num / total).T
        if e:
            n = out.shape[0]
            scale = scale_of(result)
            done[head_at(e), 0:n] = code_of(result, scale.astype(jnp.float32))
            done[head_at(e), n:n + EXTRA] = jnp.broadcast_to(scale, (EXTRA, HEAD))
            done_copy(e, done, back, send, recv).start()
        else:
            out[:, own_lanes] = result

    last = [d % HEADS for d in range(1, HEADS + 1)]

    def finish_a(e):
        h = head_at(e)
        parts = [part_of(part_a.at[k, h])]
        for d in range(1, K):
            kk = (k + d) % K
            remote(
                code_a.at[kk, h], got_a.at[kk, h], part_a_send.at[d, e], got_a_recv.at[kk, h],
                at_k(d),
            ).wait_recv()
            parts.append(sent_part_of(got_a.at[kk, h]))
        finish(e, parts, done_a, back_a, out_a, done_a_send, done_a_recv)

    blocks = 2 * Q
    for i in range(blocks):
        d = order[i % Q]
        if i < Q:
            col_block((q + d) % Q * 2 + 1 - c)
            mate_b_copy(d).start()
        else:
            col_block((q + d) % Q * 2 + c)
        for e in last[i * HEADS // blocks:(i + 1) * HEADS // blocks]:
            finish_a(e)

    for d in order:
        qq = (q + d) % Q
        mate_b_copy(d).wait_recv()
        for e in range(HEADS):
            h = head_at(e)
            both = merged([part_of(part_b.at[qq * 2 + c, h]), part_of(mate_b.at[qq, h])])
            if d:
                codes, extra = packed_part(*both)
                code_b[qq, h, 0:HEAD] = codes
                code_b[qq, h, HEAD:HEAD + EXTRA] = extra
                part_b_copy(d, e).start()
            else:
                part_b[qq * 2 + c, h, 0:HEAD] = both[0]
                part_b[qq * 2 + c, h, HEAD:HEAD + 1] = both[2]
                part_b[qq * 2 + c, h, HEAD + 1:HEAD + 2] = both[1]

    for e in last:
        h = head_at(e)
        parts = [part_of(part_b.at[s, h])]
        for d in range(1, Q):
            qq = (q + d) % Q
            remote(
                code_b.at[qq, h], got_b.at[qq, h], part_b_send.at[d, e],
                got_b_recv.at[qq, h], at_q(d),
            ).wait_recv()
            parts.append(sent_part_of(got_b.at[qq, h]))
        finish(e, parts, done_b, back_b, out_b, done_b_send, done_b_recv)

    for e in range(1, HEADS):
        take_done(e, done_a, back_a, out_a, done_a_send, done_a_recv)
    for e in range(1, HEADS):
        take_done(e, done_b, back_b, out_b, done_b_send, done_b_recv)

    for d in range(1, HEADS):
        for i in range(2):
            cut_b_copy(d, i).wait_send()
            cut_a_copy(d, i).wait_send()
    for e in range(HEADS):
        for d in range(1, K):
            a_copy(d, e).wait_send()
            part_a_copy(d, e).wait_send()
        for d in range(Q):
            if d:
                b_copy(d, e).wait_send()
                part_b_copy(d, e).wait_send()
            mate_copy(d, e).wait_send()
    for d in range(Q):
        mate_b_copy(d).wait_send()
    for e in range(1, HEADS):
        done_copy(e, done_a, back_a, done_a_send, done_a_recv).wait_send()
        done_copy(e, done_b, back_b, done_b_send, done_b_recv).wait_send()


def on_device(rows, cols, rep_a, val_a, rep_b, val_b):
    Q, K = rows // HEADS, cols // 2
    n_a, n_b = rep_a.shape[0], rep_b.shape[0]
    f32, bf16 = jnp.float32, jnp.bfloat16
    tall = HEAD + STATS
    dma = pltpu.SemaphoreType.DMA
    vmem = pl.BlockSpec(memory_space=pltpu.VMEM)
    hbm = pl.BlockSpec(memory_space=pltpu.HBM)
    tile = K * HEADS * n_a * 2 * Q * HEADS * n_b
    return pl.pallas_call(
        functools.partial(kernel, rows, cols),
        out_shape=(
            jax.ShapeDtypeStruct(rep_a.shape, f32),
            jax.ShapeDtypeStruct(rep_b.shape, f32),
        ),
        in_specs=[hbm] * 4,
        out_specs=(vmem, vmem),
        scratch_shapes=[
            pltpu.VMEM((HEADS, K, 2, n_a, HEAD), bf16),
            pltpu.VMEM((2 * Q, HEADS, 2, n_b, HEAD), bf16),
            pltpu.VMEM((2 * Q, HEAD, HEADS * n_b), bf16),
            pltpu.VMEM((2 * Q, K * HEADS * n_a, HEADS * n_b), f32),
            pltpu.VMEM((2 * Q, 1, HEADS * n_b), f32),
            pltpu.VMEM((K, HEADS, tall, n_a), f32),
            pltpu.VMEM((K, HEADS, HEAD + EXTRA, n_a), bf16),
            pltpu.VMEM((K, HEADS, HEAD + EXTRA, n_a), bf16),
            pltpu.VMEM((2 * Q, HEADS, tall, n_b), f32),
            pltpu.VMEM((Q, HEADS, tall, n_b), f32),
            pltpu.VMEM((Q, HEADS, HEAD + EXTRA, n_b), bf16),
            pltpu.VMEM((Q, HEADS, HEAD + EXTRA, n_b), bf16),
            pltpu.VMEM((HEADS, n_a + EXTRA, HEAD), bf16),
            pltpu.VMEM((HEADS, n_b + EXTRA, HEAD), bf16),
            pltpu.VMEM((HEADS, n_a + EXTRA, HEAD), bf16),
            pltpu.VMEM((HEADS, n_b + EXTRA, HEAD), bf16),
            dma((4,)), dma((HEADS, 2)), dma((HEADS, 2)),
            dma((K, HEADS)), dma((2 * Q, HEADS)),
            dma((K, HEADS)), dma((Q, HEADS)), dma((Q, HEADS)),
            dma((K, HEADS)), dma((K, HEADS)),
            dma((Q,)), dma((Q,)),
            dma((Q, HEADS)), dma((Q, HEADS)),
            dma((HEADS,)), dma((HEADS,)), dma((HEADS,)), dma((HEADS,)),
        ],
        compiler_params=pltpu.CompilerParams(
            collective_id=0, has_side_effects=True, vmem_limit_bytes=127 * 512 * 1024
        ),
        cost_estimate=pl.CostEstimate(
            flops=6 * tile * HEAD, bytes_accessed=6 * 1024 * (n_a + n_b), transcendentals=2 * tile
        ),
    )(rep_a, val_a, rep_b, val_b)


def solution(mesh):
    rows, cols = mesh.shape["row"], mesh.shape["col"]
    placed = P(("row", "col"), None)
    return jax.shard_map(
        functools.partial(on_device, rows, cols),
        mesh=mesh,
        in_specs=(placed,) * 4,
        out_specs=(placed, placed),
        check_vma=False,
    )
```

```python
import functools
import math

import jax
import jax.numpy as jnp
from jax import lax
from jax.experimental import pallas as pl
from jax.experimental.pallas import tpu as pltpu
from jax.sharding import PartitionSpec as P

HEADS = 4
HEAD = 128
STATS = 8
EXTRA = 16
BINADES = 248.0
MESH = pl.DeviceIdType.MESH


def code_of(x, scale):
    code = jnp.exp2(jnp.abs(x) * (BINADES / scale) - BINADES / 2)
    return jnp.where(x < 0, -code, code).astype(jnp.bfloat16)


def value_of(code, scale):
    code = code.astype(jnp.float32)
    size = jnp.log(jnp.abs(code)) * (1 / (math.log(2) * BINADES)) + 0.5
    return jnp.where(code < 0, -size, size) * scale


def scale_of(x):
    largest = jnp.max(jnp.abs(x), axis=0, keepdims=True) * 1.01 + 1e-30
    return largest.astype(jnp.bfloat16)


def three_terms(x):
    terms = []
    for _ in range(3):
        term = x.astype(jnp.bfloat16).astype(jnp.float32)
        terms.append(term)
        x = x - term
    return terms


def packed_part(num, total, peak):
    mean = num / total
    scale = scale_of(mean).astype(jnp.float32)
    rows = [scale] + three_terms(peak) + three_terms(total)
    sub = lax.broadcasted_iota(jnp.int32, (EXTRA, num.shape[1]), 0)
    extra = jnp.zeros((EXTRA, num.shape[1]), jnp.float32)
    for i, x in enumerate(rows):
        extra = jnp.where(sub == i, x, extra)
    return code_of(mean, scale), extra.astype(jnp.bfloat16)


def unpacked_part(codes, extra):
    extra = extra.astype(jnp.float32)
    peak = extra[1:2] + extra[2:3] + extra[3:4]
    total = extra[4:5] + extra[5:6] + extra[6:7]
    return value_of(codes, extra[0:1]) * total, total, peak


def merged(parts):
    peak = functools.reduce(jnp.maximum, [x[2] for x in parts])
    scales = [jnp.exp2(x[2] - peak) for x in parts]
    num = sum(x[0] * w for x, w in zip(parts, scales))
    total = sum(x[1] * w for x, w in zip(parts, scales))
    return num, total, peak


def kernel(
    rows, cols,
    rep_a, val_a, rep_b, val_b, out_a, out_b,
    in_a, in_b, keys_t, scores, peak_a, peak_b,
    part_a, code_a, got_a, part_b, mate_b, code_b, got_b, done_a, done_b, back_a, back_b,
    own, cut_a_send, cut_b_send, a_recv, b_recv, a_send, b_send, mate_send,
    part_a_send, got_a_recv, mate_b_send, mate_b_recv, part_b_send, got_b_recv,
    done_a_send, done_b_send, done_a_recv, done_b_recv,
):
    Q, K = rows // HEADS, cols // 2
    n_a, n_b = rep_a.shape[0], rep_b.shape[0]
    row, col = lax.axis_index("row"), lax.axis_index("col")
    p, q = row // Q, row % Q
    k, c = col // 2, col % 2
    s = q * 2 + c
    to_log2 = HEAD ** -0.5 * math.log2(math.e)

    def head_at(d):
        return (p + d) % HEADS

    def at_head(d):
        return (head_at(d) * Q + q, col)

    def at_k(d):
        return (row, (k + d) % K * 2 + c)

    def at_q(d):
        return (p * Q + (q + d) % Q, col)

    mate = (row, k * 2 + 1 - c)

    def remote(src, dst, send, recv, device):
        return pltpu.make_async_remote_copy(
            src_ref=src, dst_ref=dst, send_sem=send, recv_sem=recv,
            device_id=device, device_id_type=MESH,
        )

    barrier = pltpu.get_barrier_semaphore()
    peers = [at_head(d) for d in range(1, HEADS)] + [at_k(d) for d in range(1, K)]
    peers += [at_q(d) for d in range(1, Q)] + [mate]
    for peer in peers:
        pl.semaphore_signal(barrier, inc=1, device_id=peer, device_id_type=MESH)

    def head_lanes(h):
        return pl.ds(pl.multiple_of(h * HEAD, HEAD), HEAD)

    own_lanes = head_lanes(p)
    own_copies = [
        pltpu.make_async_copy(x.at[:, own_lanes], y, own.at[i])
        for i, (x, y) in enumerate([
            (rep_b, in_b.at[s, p, 0]), (val_b, in_b.at[s, p, 1]),
            (rep_a, in_a.at[p, k, 0]), (val_a, in_a.at[p, k, 1]),
        ])
    ]
    for copy in own_copies:
        copy.start()
    peak_b[...] = jnp.full_like(peak_b, -jnp.inf)
    pl.semaphore_wait(barrier, len(peers))

    def cut_b_copy(d, i):
        return remote(
            (rep_b, val_b)[i].at[:, head_lanes(head_at(d))], in_b.at[s, p, i],
            cut_b_send.at[d, i], b_recv.at[s, p, i], at_head(d),
        )

    def cut_a_copy(d, i):
        return remote(
            (rep_a, val_a)[i].at[:, head_lanes(head_at(d))], in_a.at[p, k, i],
            cut_a_send.at[d, i], a_recv.at[k, p, i], at_head(d),
        )

    def a_copy(d, e, i):
        h = head_at(e)
        piece = in_a.at[h, k, i]
        return remote(piece, piece, a_send.at[d, e, i], a_recv.at[k, h, i], at_k(d))

    def b_copy(d, e, i):
        h = head_at(e)
        piece = in_b.at[s, h, i]
        return remote(piece, piece, b_send.at[d, e, i], b_recv.at[s, h, i], at_q(d))

    def mate_copy(d, e, i):
        r, h = (q + d) % Q * 2 + c, head_at(e)
        piece = in_b.at[r, h, i]
        return remote(piece, piece, mate_send.at[d, e, i], b_recv.at[r, h, i], mate)

    def wait_b(r, e, i, device):
        h = head_at(e)
        piece = in_b.at[r, h, i]
        remote(piece, piece, mate_send.at[0, 0, i], b_recv.at[r, h, i], device).wait_recv()

    def wait_a(r, e, i, device):
        h = head_at(e)
        piece = in_a.at[h, r, i]
        remote(piece, piece, mate_send.at[0, 0, i], a_recv.at[r, h, i], device).wait_recv()

    def pass_b(e, i):
        if e:
            wait_b(s, e, i, at_head(e))
        for d in range(1, Q):
            b_copy(d, e, i).start()
        mate_copy(0, e, i).start()

    def pass_b_to_mate(e, i):
        for d in range(1, Q):
            wait_b((q + d) % Q * 2 + c, e, i, at_q(d))
            mate_copy(d, e, i).start()

    def end_b(e, i):
        for d in range(Q):
            wait_b((q + d) % Q * 2 + 1 - c, e, i, mate)

    def pass_a(e, i):
        if e:
            wait_a(k, e, i, at_head(e))
        for d in range(1, K):
            a_copy(d, e, i).start()

    def end_a(e, i):
        for d in range(1, K):
            wait_a((k + d) % K, e, i, at_k(d))

    heads = range(HEADS)
    for cut, i in ((cut_b_copy, 0), (cut_a_copy, 0), (cut_a_copy, 1), (cut_b_copy, 1)):
        for d in range(1, HEADS):
            cut(d, i).start()
    for copy in own_copies:
        copy.wait()
    pass_b(0, 0)
    pass_a(0, 0)
    pass_a(0, 1)
    for e in range(1, HEADS):
        pass_b(e, 0)
        pass_b_to_mate(e - 1, 0)
    pass_b(0, 1)
    pass_a(1, 0)
    pass_b_to_mate(HEADS - 1, 0)

    width = HEADS * n_b
    span = K * n_a
    for d in range(Q):
        r = (q + d) % Q * 2 + c
        keys_t[r] = in_b[r, :, 0].reshape(width, HEAD).T
    for e in heads:
        end_b(e, 0)
    for d in range(Q):
        r = (q + d) % Q * 2 + 1 - c
        keys_t[r] = in_b[r, :, 0].reshape(width, HEAD).T

    def rows_at(e):
        return pl.ds(pl.multiple_of(head_at(e) * span, span), span)

    def lane_groups(x):
        return [x[:, j:j + HEAD] for j in range(0, width, HEAD)]

    def score_block(e):
        queries = in_a[head_at(e), :, 0].reshape(span, HEAD)
        peak = jnp.full((span, HEAD), -jnp.inf, jnp.float32)
        for r in range(2 * Q):
            logits = jnp.dot(queries, keys_t[r], preferred_element_type=jnp.float32) * to_log2
            scores[r, rows_at(e), :] = logits
            tops = jnp.max(logits.reshape(span // 8, 8, width), axis=0)
            peak_b[r] = jnp.maximum(peak_b[r], tops)
            peak = functools.reduce(jnp.maximum, lane_groups(logits), peak)
        peak_a[e] = peak

    for e in heads:
        if e + 1 < HEADS:
            if e:
                pass_a(e + 1, 0)
        end_a(e, 0)
        score_block(e)
        if e:
            pass_a(e, 1)

    def row_block(e):
        pp = head_at(e)
        peak = jnp.max(peak_a[e], axis=1, keepdims=True)
        totals = jnp.zeros((span, HEAD), jnp.float32)
        num = jnp.zeros((span, HEAD), jnp.float32)
        for r in range(2 * Q):
            values = in_b[r, :, 1].reshape(width, HEAD)
            weights = jnp.exp2(scores[r, rows_at(e), :] - peak)
            totals = functools.reduce(jnp.add, lane_groups(weights), totals)
            num += jnp.dot(
                weights.astype(jnp.bfloat16), values, preferred_element_type=jnp.float32
            )
        total = jnp.sum(totals, axis=1, keepdims=True)
        lane = lax.broadcasted_iota(jnp.int32, (span, HEAD), 1)
        stats = jnp.where(lane == 0, peak, total)
        for kk in range(K):
            mine = slice(kk * n_a, (kk + 1) * n_a)
            num_t = num[mine].T
            stats_t = stats[mine].T[0:STATS]
            part_a[kk, pp, 0:HEAD] = num_t
            part_a[kk, pp, HEAD:HEAD + STATS] = stats_t
            codes, extra = packed_part(num_t, stats_t[1:2], stats_t[0:1])
            code_a[kk, pp, 0:HEAD] = codes
            code_a[kk, pp, HEAD:HEAD + EXTRA] = extra

    def part_a_copy(d, e):
        there = (k + d) % K
        h = head_at(e)
        return remote(
            code_a.at[there, h], got_a.at[k, h], part_a_send.at[d, e], got_a_recv.at[k, h], at_k(d)
        )

    for e in heads:
        end_a(e, 1)
    values_t = in_a[:, :, 1].reshape(HEADS * span, HEAD).T

    def col_block(r):
        peak = jnp.max(peak_b[r], axis=0, keepdims=True)
        weights = jnp.exp2(scores[r] - peak)
        total = jnp.sum(weights, axis=0, keepdims=True)
        num = jnp.dot(values_t, weights.astype(jnp.bfloat16), preferred_element_type=jnp.float32)
        sub = lax.broadcasted_iota(jnp.int32, (STATS, width), 0)
        stats = jnp.where(sub == 0, peak, total)
        for h in range(HEADS):
            part_b[r, h, 0:HEAD] = num[:, h * n_b:(h + 1) * n_b]
            part_b[r, h, HEAD:HEAD + STATS] = stats[:, h * n_b:(h + 1) * n_b]

    def mate_b_copy(d):
        qq = (q + d) % Q
        return remote(
            part_b.at[qq * 2 + 1 - c], mate_b.at[qq], mate_b_send.at[d], mate_b_recv.at[qq], mate
        )

    def part_b_copy(d, e):
        h = head_at(e)
        return remote(
            code_b.at[(q + d) % Q, h], got_b.at[q, h], part_b_send.at[d, e], got_b_recv.at[q, h], at_q(d)
        )

    order = [d % Q for d in range(1, Q + 1)]

    def part_of(ref):
        return ref[0:HEAD], ref[HEAD + 1:HEAD + 2], ref[HEAD:HEAD + 1]

    def sent_part_of(ref):
        return unpacked_part(ref[0:HEAD], ref[HEAD:HEAD + EXTRA])

    def done_copy(e, done, back, send, recv):
        return remote(done.at[head_at(e)], back.at[p], send.at[e], recv.at[p], at_head(e))

    def take_done(e, done, back, out, send, recv):
        h = head_at(e)
        remote(done.at[h], back.at[h], send.at[e], recv.at[h], at_head(e)).wait_recv()
        n = out.shape[0]
        scale = back[h, n:n + EXTRA].astype(jnp.float32)[0:1]
        out[:, head_lanes(h)] = value_of(back[h, 0:n], scale)

    def finish(e, parts, done, back, out, send, recv):
        num, total, _ = merged(parts)
        result = (num / total).T
        if e:
            n = out.shape[0]
            scale = scale_of(result)
            done[head_at(e), 0:n] = code_of(result, scale.astype(jnp.float32))
            done[head_at(e), n:n + EXTRA] = jnp.broadcast_to(scale, (EXTRA, HEAD))
            done_copy(e, done, back, send, recv).start()
        else:
            out[:, own_lanes] = result

    last = [d % HEADS for d in range(1, HEADS + 1)]

    def finish_a(e):
        h = head_at(e)
        parts = [part_of(part_a.at[k, h])]
        for d in range(1, K):
            kk = (k + d) % K
            remote(
                code_a.at[kk, h], got_a.at[kk, h], part_a_send.at[d, e], got_a_recv.at[kk, h],
                at_k(d),
            ).wait_recv()
            parts.append(sent_part_of(got_a.at[kk, h]))
        finish(e, parts, done_a, back_a, out_a, done_a_send, done_a_recv)

    def finish_b(e):
        h = head_at(e)
        parts = [part_of(part_b.at[s, h])]
        for d in range(1, Q):
            qq = (q + d) % Q
            remote(
                code_b.at[qq, h], got_b.at[qq, h], part_b_send.at[d, e],
                got_b_recv.at[qq, h], at_q(d),
            ).wait_recv()
            parts.append(sent_part_of(got_b.at[qq, h]))
        finish(e, parts, done_b, back_b, out_b, done_b_send, done_b_recv)

    def merge_mate(d):
        qq = (q + d) % Q
        mate_b_copy(d).wait_recv()
        for e in range(HEADS):
            h = head_at(e)
            both = merged([part_of(part_b.at[qq * 2 + c, h]), part_of(mate_b.at[qq, h])])
            if d:
                codes, extra = packed_part(*both)
                code_b[qq, h, 0:HEAD] = codes
                code_b[qq, h, HEAD:HEAD + EXTRA] = extra
                part_b_copy(d, e).start()
            else:
                part_b[qq * 2 + c, h, 0:HEAD] = both[0]
                part_b[qq * 2 + c, h, HEAD:HEAD + 1] = both[2]
                part_b[qq * 2 + c, h, HEAD + 1:HEAD + 2] = both[1]

    for n, d in enumerate(order):
        col_block((q + d) % Q * 2 + 1 - c)
        mate_b_copy(d).start()
        if n == 0:
            for e in range(1, HEADS):
                pass_b(e, 1)
    for e in heads:
        pass_b_to_mate(e, 1)
    for d in order:
        col_block((q + d) % Q * 2 + c)
        merge_mate(d)
    for e in heads:
        end_b(e, 1)

    for n, e in enumerate(last):
        row_block(e)
        for d in range(1, K):
            part_a_copy(d, e).start()
        if n:
            finish_a(last[n - 1])
        finish_b(e)
    finish_a(last[-1])
    for e in range(1, HEADS):
        take_done(e, done_b, back_b, out_b, done_b_send, done_b_recv)
    for e in range(1, HEADS):
        take_done(e, done_a, back_a, out_a, done_a_send, done_a_recv)

    for d in range(1, HEADS):
        for i in range(2):
            cut_b_copy(d, i).wait_send()
            cut_a_copy(d, i).wait_send()
    for e in range(HEADS):
        for d in range(1, K):
            for i in range(2):
                a_copy(d, e, i).wait_send()
            part_a_copy(d, e).wait_send()
        for d in range(Q):
            if d:
                for i in range(2):
                    b_copy(d, e, i).wait_send()
                part_b_copy(d, e).wait_send()
            for i in range(2):
                mate_copy(d, e, i).wait_send()
    for d in range(Q):
        mate_b_copy(d).wait_send()
    for e in range(1, HEADS):
        done_copy(e, done_a, back_a, done_a_send, done_a_recv).wait_send()
        done_copy(e, done_b, back_b, done_b_send, done_b_recv).wait_send()


def on_device(rows, cols, rep_a, val_a, rep_b, val_b):
    Q, K = rows // HEADS, cols // 2
    n_a, n_b = rep_a.shape[0], rep_b.shape[0]
    f32, bf16 = jnp.float32, jnp.bfloat16
    tall = HEAD + STATS
    dma = pltpu.SemaphoreType.DMA
    vmem = pl.BlockSpec(memory_space=pltpu.VMEM)
    hbm = pl.BlockSpec(memory_space=pltpu.HBM)
    tile = K * HEADS * n_a * 2 * Q * HEADS * n_b
    return pl.pallas_call(
        functools.partial(kernel, rows, cols),
        out_shape=(
            jax.ShapeDtypeStruct(rep_a.shape, f32),
            jax.ShapeDtypeStruct(rep_b.shape, f32),
        ),
        in_specs=[hbm] * 4,
        out_specs=(vmem, vmem),
        scratch_shapes=[
            pltpu.VMEM((HEADS, K, 2, n_a, HEAD), bf16),
            pltpu.VMEM((2 * Q, HEADS, 2, n_b, HEAD), bf16),
            pltpu.VMEM((2 * Q, HEAD, HEADS * n_b), bf16),
            pltpu.VMEM((2 * Q, K * HEADS * n_a, HEADS * n_b), f32),
            pltpu.VMEM((HEADS, K * n_a, HEAD), f32),
            pltpu.VMEM((2 * Q, 8, HEADS * n_b), f32),
            pltpu.VMEM((K, HEADS, tall, n_a), f32),
            pltpu.VMEM((K, HEADS, HEAD + EXTRA, n_a), bf16),
            pltpu.VMEM((K, HEADS, HEAD + EXTRA, n_a), bf16),
            pltpu.VMEM((2 * Q, HEADS, tall, n_b), f32),
            pltpu.VMEM((Q, HEADS, tall, n_b), f32),
            pltpu.VMEM((Q, HEADS, HEAD + EXTRA, n_b), bf16),
            pltpu.VMEM((Q, HEADS, HEAD + EXTRA, n_b), bf16),
            pltpu.VMEM((HEADS, n_a + EXTRA, HEAD), bf16),
            pltpu.VMEM((HEADS, n_b + EXTRA, HEAD), bf16),
            pltpu.VMEM((HEADS, n_a + EXTRA, HEAD), bf16),
            pltpu.VMEM((HEADS, n_b + EXTRA, HEAD), bf16),
            dma((4,)), dma((HEADS, 2)), dma((HEADS, 2)),
            dma((K, HEADS, 2)), dma((2 * Q, HEADS, 2)),
            dma((K, HEADS, 2)), dma((Q, HEADS, 2)), dma((Q, HEADS, 2)),
            dma((K, HEADS)), dma((K, HEADS)),
            dma((Q,)), dma((Q,)),
            dma((Q, HEADS)), dma((Q, HEADS)),
            dma((HEADS,)), dma((HEADS,)), dma((HEADS,)), dma((HEADS,)),
        ],
        compiler_params=pltpu.CompilerParams(
            collective_id=0, has_side_effects=True, vmem_limit_bytes=127 * 512 * 1024
        ),
        cost_estimate=pl.CostEstimate(
            flops=6 * tile * HEAD, bytes_accessed=6 * 1024 * (n_a + n_b), transcendentals=2 * tile
        ),
    )(rep_a, val_a, rep_b, val_b)


def solution(mesh):
    rows, cols = mesh.shape["row"], mesh.shape["col"]
    placed = P(("row", "col"), None)
    return jax.shard_map(
        functools.partial(on_device, rows, cols),
        mesh=mesh,
        in_specs=(placed,) * 4,
        out_specs=(placed, placed),
        check_vma=False,
    )
```

```python
import functools
import math

import jax
import jax.numpy as jnp
from jax import lax
from jax.experimental import pallas as pl
from jax.experimental.pallas import tpu as pltpu
from jax.sharding import PartitionSpec as P

HEADS = 4
HEAD = 128
STATS = 8
EXTRA = 16
BINADES = 248.0
MESH = pl.DeviceIdType.MESH


def code_of(x, scale):
    code = jnp.exp2(jnp.abs(x) * (BINADES / scale) - BINADES / 2)
    return jnp.where(x < 0, -code, code).astype(jnp.bfloat16)


def value_of(code, scale):
    code = code.astype(jnp.float32)
    size = jnp.log(jnp.abs(code)) * (1 / (math.log(2) * BINADES)) + 0.5
    return jnp.where(code < 0, -size, size) * scale


def scale_of(x):
    largest = jnp.max(jnp.abs(x), axis=0, keepdims=True) * 1.01 + 1e-30
    return largest.astype(jnp.bfloat16)


def three_terms(x):
    terms = []
    for _ in range(3):
        term = x.astype(jnp.bfloat16).astype(jnp.float32)
        terms.append(term)
        x = x - term
    return terms


def packed_part(num, total, peak):
    mean = num / total
    scale = scale_of(mean).astype(jnp.float32)
    rows = [scale] + three_terms(peak) + three_terms(total)
    sub = lax.broadcasted_iota(jnp.int32, (EXTRA, num.shape[1]), 0)
    extra = jnp.zeros((EXTRA, num.shape[1]), jnp.float32)
    for i, x in enumerate(rows):
        extra = jnp.where(sub == i, x, extra)
    return code_of(mean, scale), extra.astype(jnp.bfloat16)


def unpacked_part(codes, extra):
    extra = extra.astype(jnp.float32)
    peak = extra[1:2] + extra[2:3] + extra[3:4]
    total = extra[4:5] + extra[5:6] + extra[6:7]
    return value_of(codes, extra[0:1]) * total, total, peak


def merged(parts):
    peak = functools.reduce(jnp.maximum, [x[2] for x in parts])
    scales = [jnp.exp2(x[2] - peak) for x in parts]
    num = sum(x[0] * w for x, w in zip(parts, scales))
    total = sum(x[1] * w for x, w in zip(parts, scales))
    return num, total, peak


def kernel(
    rows, cols,
    rep_a, val_a, rep_b, val_b, out_a, out_b,
    in_a, in_b, keys_t, values_t, scores, peak_a, peak_b,
    part_a, code_a, got_a, part_b, mate_b, code_b, got_b, done_a, done_b, back_a, back_b,
    own, cut_a_send, cut_b_send, a_recv, b_recv, a_send, b_send, mate_send,
    part_a_send, got_a_recv, mate_b_send, mate_b_recv, part_b_send, got_b_recv,
    done_a_send, done_b_send, done_a_recv, done_b_recv,
):
    Q, K = rows // HEADS, cols // 2
    n_a, n_b = rep_a.shape[0], rep_b.shape[0]
    row, col = lax.axis_index("row"), lax.axis_index("col")
    p, q = lax.div(row, Q), lax.rem(row, Q)
    k, c = lax.div(col, 2), lax.rem(col, 2)
    s = q * 2 + c
    to_log2 = HEAD ** -0.5 * math.log2(math.e)

    def head_at(d):
        return lax.rem(p + d, HEADS)

    def at_head(d):
        return (head_at(d) * Q + q, col)

    def at_k(d):
        return (row, lax.rem(k + d, K) * 2 + c)

    def at_q(d):
        return (p * Q + lax.rem(q + d, Q), col)

    mate = (row, k * 2 + 1 - c)

    def remote(src, dst, send, recv, device):
        return pltpu.make_async_remote_copy(
            src_ref=src, dst_ref=dst, send_sem=send, recv_sem=recv,
            device_id=device, device_id_type=MESH,
        )

    barrier = pltpu.get_barrier_semaphore()
    peers = [at_head(d) for d in range(1, HEADS)] + [at_k(d) for d in range(1, K)]
    peers += [at_q(d) for d in range(1, Q)] + [mate]
    for peer in peers:
        pl.semaphore_signal(barrier, inc=1, device_id=peer, device_id_type=MESH)

    def head_lanes(h):
        return pl.ds(pl.multiple_of(h * HEAD, HEAD), HEAD)

    own_lanes = head_lanes(p)
    own_copies = [
        pltpu.make_async_copy(x.at[:, own_lanes], y, own.at[i])
        for i, (x, y) in enumerate([
            (rep_b, in_b.at[s, p, 0]), (val_b, in_b.at[s, p, 1]),
            (rep_a, in_a.at[p, k, 0]), (val_a, in_a.at[p, k, 1]),
        ])
    ]
    for copy in own_copies:
        copy.start()
    peak_b[...] = jnp.full_like(peak_b, -jnp.inf)
    pl.semaphore_wait(barrier, len(peers))

    def cut_b_copy(d, i):
        return remote(
            (rep_b, val_b)[i].at[:, head_lanes(head_at(d))], in_b.at[s, p, i],
            cut_b_send.at[d, i], b_recv.at[s, p, i], at_head(d),
        )

    def cut_a_copy(d, i):
        return remote(
            (rep_a, val_a)[i].at[:, head_lanes(head_at(d))], in_a.at[p, k, i],
            cut_a_send.at[d, i], a_recv.at[k, p, i], at_head(d),
        )

    def a_copy(d, e, i):
        h = head_at(e)
        piece = in_a.at[h, k, i]
        return remote(piece, piece, a_send.at[d, e, i], a_recv.at[k, h, i], at_k(d))

    def b_copy(d, e, i):
        h = head_at(e)
        piece = in_b.at[s, h, i]
        return remote(piece, piece, b_send.at[d, e, i], b_recv.at[s, h, i], at_q(d))

    def mate_copy(d, e, i):
        r, h = lax.rem(q + d, Q) * 2 + c, head_at(e)
        piece = in_b.at[r, h, i]
        return remote(piece, piece, mate_send.at[d, e, i], b_recv.at[r, h, i], mate)

    def wait_b(r, e, i, device):
        h = head_at(e)
        piece = in_b.at[r, h, i]
        remote(piece, piece, mate_send.at[0, 0, i], b_recv.at[r, h, i], device).wait_recv()

    def wait_a(r, e, i, device):
        h = head_at(e)
        piece = in_a.at[h, r, i]
        remote(piece, piece, mate_send.at[0, 0, i], a_recv.at[r, h, i], device).wait_recv()

    def pass_b(e, i, own=False):
        if not own:
            wait_b(s, e, i, at_head(e))
        for d in range(1, Q):
            b_copy(d, e, i).start()
        mate_copy(0, e, i).start()

    def pass_b_to_mate(e, i):
        for d in range(1, Q):
            wait_b(lax.rem(q + d, Q) * 2 + c, e, i, at_q(d))
            mate_copy(d, e, i).start()

    def end_b(e, i):
        for d in range(Q):
            wait_b(lax.rem(q + d, Q) * 2 + 1 - c, e, i, mate)

    def pass_a(e, i, own=False):
        if not own:
            wait_a(k, e, i, at_head(e))
        for d in range(1, K):
            a_copy(d, e, i).start()

    def end_a(e, i):
        for d in range(1, K):
            wait_a(lax.rem(k + d, K), e, i, at_k(d))

    for cut, i in ((cut_b_copy, 0), (cut_a_copy, 0), (cut_a_copy, 1), (cut_b_copy, 1)):
        pl.loop(1, HEADS)(lambda d, cut=cut, i=i: cut(d, i).start())
    for copy in own_copies:
        copy.wait()
    for i in range(2):
        pass_b(0, i, own=True)
        pass_a(0, i, own=True)

    @pl.loop(1, HEADS)
    def _(e):
        pass_b(e, 0)
        pass_b_to_mate(e - 1, 0)

    pass_b_to_mate(HEADS - 1, 0)
    pl.loop(1, HEADS)(lambda e: pass_a(e, 0))

    width = HEADS * n_b
    span = K * n_a
    pl.loop(0, HEADS)(lambda e: end_b(e, 0))

    @pl.loop(0, 2 * Q)
    def _(r):
        keys_t[r] = in_b[r, :, 0].reshape(width, HEAD).T

    def rows_at(e):
        return pl.ds(pl.multiple_of(head_at(e) * span, span), span)

    def lane_groups(x):
        return [x[:, j:j + HEAD] for j in range(0, width, HEAD)]

    def score_block(e):
        queries = in_a[head_at(e), :, 0].reshape(span, HEAD)
        peak = jnp.full((span, HEAD), -jnp.inf, jnp.float32)
        for r in range(2 * Q):
            logits = jnp.dot(queries, keys_t[r], preferred_element_type=jnp.float32) * to_log2
            scores[r, rows_at(e), :] = logits
            tops = jnp.max(logits.reshape(span // 8, 8, width), axis=0)
            peak_b[r] = jnp.maximum(peak_b[r], tops)
            peak = functools.reduce(jnp.maximum, lane_groups(logits), peak)
        peak_a[e] = peak

    @pl.loop(0, HEADS)
    def _(e):
        end_a(e, 0)
        score_block(e)

        @pl.when(e > 0)
        def _():
            pass_a(e, 1)

    def row_block(e):
        pp = head_at(e)
        peak = jnp.max(peak_a[e], axis=1, keepdims=True)
        totals = jnp.zeros((span, HEAD), jnp.float32)
        num = jnp.zeros((span, HEAD), jnp.float32)
        for r in range(2 * Q):
            values = in_b[r, :, 1].reshape(width, HEAD)
            weights = jnp.exp2(scores[r, rows_at(e), :] - peak)
            totals = functools.reduce(jnp.add, lane_groups(weights), totals)
            num += jnp.dot(
                weights.astype(jnp.bfloat16), values, preferred_element_type=jnp.float32
            )
        total = jnp.sum(totals, axis=1, keepdims=True)
        lane = lax.broadcasted_iota(jnp.int32, (span, HEAD), 1)
        stats = jnp.where(lane == 0, peak, total)
        for kk in range(K):
            mine = slice(kk * n_a, (kk + 1) * n_a)
            num_t = num[mine].T
            stats_t = stats[mine].T[0:STATS]
            part_a[kk, pp, 0:HEAD] = num_t
            part_a[kk, pp, HEAD:HEAD + STATS] = stats_t
            codes, extra = packed_part(num_t, stats_t[1:2], stats_t[0:1])
            code_a[kk, pp, 0:HEAD] = codes
            code_a[kk, pp, HEAD:HEAD + EXTRA] = extra

    def part_a_copy(d, e):
        there = lax.rem(k + d, K)
        h = head_at(e)
        return remote(
            code_a.at[there, h], got_a.at[k, h], part_a_send.at[d, e], got_a_recv.at[k, h], at_k(d)
        )

    pl.loop(0, HEADS)(lambda e: end_a(e, 1))
    values_t[...] = in_a[:, :, 1].reshape(HEADS * span, HEAD).T

    def col_block(r):
        peak = jnp.max(peak_b[r], axis=0, keepdims=True)
        weights = jnp.exp2(scores[r] - peak)
        total = jnp.sum(weights, axis=0, keepdims=True)
        num = jnp.dot(values_t[...], weights.astype(jnp.bfloat16), preferred_element_type=jnp.float32)
        sub = lax.broadcasted_iota(jnp.int32, (STATS, width), 0)
        stats = jnp.where(sub == 0, peak, total)
        for h in range(HEADS):
            part_b[r, h, 0:HEAD] = num[:, h * n_b:(h + 1) * n_b]
            part_b[r, h, HEAD:HEAD + STATS] = stats[:, h * n_b:(h + 1) * n_b]

    def mate_b_copy(d):
        qq = lax.rem(q + d, Q)
        return remote(
            part_b.at[qq * 2 + 1 - c], mate_b.at[qq], mate_b_send.at[d], mate_b_recv.at[qq], mate
        )

    def part_b_copy(d, e):
        h = head_at(e)
        return remote(
            code_b.at[lax.rem(q + d, Q), h], got_b.at[q, h], part_b_send.at[d, e], got_b_recv.at[q, h], at_q(d)
        )

    def part_of(ref):
        return ref[0:HEAD], ref[HEAD + 1:HEAD + 2], ref[HEAD:HEAD + 1]

    def sent_part_of(ref):
        return unpacked_part(ref[0:HEAD], ref[HEAD:HEAD + EXTRA])

    def done_copy(e, done, back, send, recv):
        return remote(done.at[head_at(e)], back.at[p], send.at[e], recv.at[p], at_head(e))

    def take_done(e, done, back, out, send, recv):
        h = head_at(e)
        remote(done.at[h], back.at[h], send.at[e], recv.at[h], at_head(e)).wait_recv()
        n = out.shape[0]
        scale = back[h, n:n + EXTRA].astype(jnp.float32)[0:1]
        out[:, head_lanes(h)] = value_of(back[h, 0:n], scale)

    def finish(e, parts, done, back, out, send, recv):
        num, total, _ = merged(parts)
        result = (num / total).T

        @pl.when(e > 0)
        def _():
            n = out.shape[0]
            scale = scale_of(result)
            done[head_at(e), 0:n] = code_of(result, scale.astype(jnp.float32))
            done[head_at(e), n:n + EXTRA] = jnp.broadcast_to(scale, (EXTRA, HEAD))
            done_copy(e, done, back, send, recv).start()

        @pl.when(e == 0)
        def _():
            out[:, own_lanes] = result

    def finish_a(e):
        h = head_at(e)
        parts = [part_of(part_a.at[k, h])]
        for d in range(1, K):
            kk = lax.rem(k + d, K)
            remote(
                code_a.at[kk, h], got_a.at[kk, h], part_a_send.at[d, e], got_a_recv.at[kk, h],
                at_k(d),
            ).wait_recv()
            parts.append(sent_part_of(got_a.at[kk, h]))
        finish(e, parts, done_a, back_a, out_a, done_a_send, done_a_recv)

    def finish_b(e):
        h = head_at(e)
        parts = [part_of(part_b.at[s, h])]
        for d in range(1, Q):
            qq = lax.rem(q + d, Q)
            remote(
                code_b.at[qq, h], got_b.at[qq, h], part_b_send.at[d, e],
                got_b_recv.at[qq, h], at_q(d),
            ).wait_recv()
            parts.append(sent_part_of(got_b.at[qq, h]))
        finish(e, parts, done_b, back_b, out_b, done_b_send, done_b_recv)

    def merge_mate(d):
        qq = lax.rem(q + d, Q)
        mate_b_copy(d).wait_recv()

        @pl.loop(0, HEADS)
        def _(e):
            h = head_at(e)
            both = merged([part_of(part_b.at[qq * 2 + c, h]), part_of(mate_b.at[qq, h])])

            @pl.when(d > 0)
            def _():
                codes, extra = packed_part(*both)
                code_b[qq, h, 0:HEAD] = codes
                code_b[qq, h, HEAD:HEAD + EXTRA] = extra
                part_b_copy(d, e).start()

            @pl.when(d == 0)
            def _():
                part_b[qq * 2 + c, h, 0:HEAD] = both[0]
                part_b[qq * 2 + c, h, HEAD:HEAD + 1] = both[2]
                part_b[qq * 2 + c, h, HEAD + 1:HEAD + 2] = both[1]

    @pl.loop(0, 2 * Q)
    def _(t):
        d = lax.rem(t + 1, Q)
        first = t < Q
        col_block(lax.rem(q + d, Q) * 2 + jnp.where(first, 1 - c, c))

        @pl.when(first)
        def _():
            mate_b_copy(d).start()

        @pl.when(t == 0)
        def _():
            pl.loop(1, HEADS)(lambda e: pass_b(e, 1))

        @pl.when(t == Q - 1)
        def _():
            pl.loop(0, HEADS)(lambda e: pass_b_to_mate(e, 1))

        @pl.when(t >= Q)
        def _():
            merge_mate(d)

    pl.loop(0, HEADS)(lambda e: end_b(e, 1))

    @pl.loop(0, HEADS + 1)
    def _(n):
        @pl.when(n < HEADS)
        def _():
            e = lax.rem(n + 1, HEADS)
            row_block(e)
            for d in range(1, K):
                part_a_copy(d, e).start()
            finish_b(e)

        @pl.when(n > 0)
        def _():
            finish_a(lax.rem(n, HEADS))

    @pl.loop(1, HEADS)
    def _(e):
        take_done(e, done_b, back_b, out_b, done_b_send, done_b_recv)

    @pl.loop(1, HEADS)
    def _(e):
        take_done(e, done_a, back_a, out_a, done_a_send, done_a_recv)

    @pl.loop(1, HEADS)
    def _(e):
        for i in range(2):
            cut_b_copy(e, i).wait_send()
            cut_a_copy(e, i).wait_send()
        done_copy(e, done_a, back_a, done_a_send, done_a_recv).wait_send()
        done_copy(e, done_b, back_b, done_b_send, done_b_recv).wait_send()

    @pl.loop(0, HEADS)
    def _(e):
        for d in range(1, K):
            for i in range(2):
                a_copy(d, e, i).wait_send()
            part_a_copy(d, e).wait_send()
        for d in range(Q):
            for i in range(2):
                if d:
                    b_copy(d, e, i).wait_send()
                mate_copy(d, e, i).wait_send()
            if d:
                part_b_copy(d, e).wait_send()

    pl.loop(0, Q)(lambda d: mate_b_copy(d).wait_send())


def on_device(rows, cols, rep_a, val_a, rep_b, val_b):
    Q, K = rows // HEADS, cols // 2
    n_a, n_b = rep_a.shape[0], rep_b.shape[0]
    f32, bf16 = jnp.float32, jnp.bfloat16
    tall = HEAD + STATS
    dma = pltpu.SemaphoreType.DMA
    vmem = pl.BlockSpec(memory_space=pltpu.VMEM)
    hbm = pl.BlockSpec(memory_space=pltpu.HBM)
    tile = K * HEADS * n_a * 2 * Q * HEADS * n_b
    return pl.pallas_call(
        functools.partial(kernel, rows, cols),
        out_shape=(
            jax.ShapeDtypeStruct(rep_a.shape, f32),
            jax.ShapeDtypeStruct(rep_b.shape, f32),
        ),
        in_specs=[hbm] * 4,
        out_specs=(vmem, vmem),
        scratch_shapes=[
            pltpu.VMEM((HEADS, K, 2, n_a, HEAD), bf16),
            pltpu.VMEM((2 * Q, HEADS, 2, n_b, HEAD), bf16),
            pltpu.VMEM((2 * Q, HEAD, HEADS * n_b), bf16),
            pltpu.VMEM((HEAD, HEADS * K * n_a), bf16),
            pltpu.VMEM((2 * Q, K * HEADS * n_a, HEADS * n_b), f32),
            pltpu.VMEM((HEADS, K * n_a, HEAD), f32),
            pltpu.VMEM((2 * Q, 8, HEADS * n_b), f32),
            pltpu.VMEM((K, HEADS, tall, n_a), f32),
            pltpu.VMEM((K, HEADS, HEAD + EXTRA, n_a), bf16),
            pltpu.VMEM((K, HEADS, HEAD + EXTRA, n_a), bf16),
            pltpu.VMEM((2 * Q, HEADS, tall, n_b), f32),
            pltpu.VMEM((Q, HEADS, tall, n_b), f32),
            pltpu.VMEM((Q, HEADS, HEAD + EXTRA, n_b), bf16),
            pltpu.VMEM((Q, HEADS, HEAD + EXTRA, n_b), bf16),
            pltpu.VMEM((HEADS, n_a + EXTRA, HEAD), bf16),
            pltpu.VMEM((HEADS, n_b + EXTRA, HEAD), bf16),
            pltpu.VMEM((HEADS, n_a + EXTRA, HEAD), bf16),
            pltpu.VMEM((HEADS, n_b + EXTRA, HEAD), bf16),
            dma((4,)), dma((HEADS, 2)), dma((HEADS, 2)),
            dma((K, HEADS, 2)), dma((2 * Q, HEADS, 2)),
            dma((K, HEADS, 2)), dma((Q, HEADS, 2)), dma((Q, HEADS, 2)),
            dma((K, HEADS)), dma((K, HEADS)),
            dma((Q,)), dma((Q,)),
            dma((Q, HEADS)), dma((Q, HEADS)),
            dma((HEADS,)), dma((HEADS,)), dma((HEADS,)), dma((HEADS,)),
        ],
        compiler_params=pltpu.CompilerParams(
            collective_id=0, has_side_effects=True, vmem_limit_bytes=127 * 512 * 1024
        ),
        cost_estimate=pl.CostEstimate(
            flops=6 * tile * HEAD, bytes_accessed=6 * 1024 * (n_a + n_b), transcendentals=2 * tile
        ),
    )(rep_a, val_a, rep_b, val_b)


def solution(mesh):
    rows, cols = mesh.shape["row"], mesh.shape["col"]
    placed = P(("row", "col"), None)
    return jax.shard_map(
        functools.partial(on_device, rows, cols),
        mesh=mesh,
        in_specs=(placed,) * 4,
        out_specs=(placed, placed),
        check_vma=False,
    )
```

```python
import functools
import math

import jax
import jax.numpy as jnp
from jax import lax
from jax.experimental import pallas as pl
from jax.experimental.pallas import tpu as pltpu
from jax.sharding import PartitionSpec as P

HEADS = 4
HEAD = 128
STATS = 8
EXTRA = 16
BINADES = 248.0
GRANT = 127 * 512 * 1024
MESH = pl.DeviceIdType.MESH


def code_of(x, scale):
    code = jnp.exp2(jnp.abs(x) * (BINADES / scale) - BINADES / 2)
    return jnp.where(x < 0, -code, code).astype(jnp.bfloat16)


def value_of(code, scale):
    code = code.astype(jnp.float32)
    size = jnp.log(jnp.abs(code)) * (1 / (math.log(2) * BINADES)) + 0.5
    return jnp.where(code < 0, -size, size) * scale


def scale_of(x):
    largest = jnp.max(jnp.abs(x), axis=0, keepdims=True) * 1.01 + 1e-30
    return largest.astype(jnp.bfloat16)


def three_terms(x):
    terms = []
    for _ in range(3):
        term = x.astype(jnp.bfloat16).astype(jnp.float32)
        terms.append(term)
        x = x - term
    return terms


def packed_part(num, total, peak):
    mean = num / total
    scale = scale_of(mean).astype(jnp.float32)
    rows = [scale] + three_terms(peak) + three_terms(total)
    sub = lax.broadcasted_iota(jnp.int32, (EXTRA, num.shape[1]), 0)
    extra = jnp.zeros((EXTRA, num.shape[1]), jnp.float32)
    for i, x in enumerate(rows):
        extra = jnp.where(sub == i, x, extra)
    return code_of(mean, scale), extra.astype(jnp.bfloat16)


def unpacked_part(codes, extra):
    extra = extra.astype(jnp.float32)
    peak = extra[1:2] + extra[2:3] + extra[3:4]
    total = extra[4:5] + extra[5:6] + extra[6:7]
    return value_of(codes, extra[0:1]) * total, total, peak


def merged(parts):
    peak = functools.reduce(jnp.maximum, [x[2] for x in parts])
    scales = [jnp.exp2(x[2] - peak) for x in parts]
    num = sum(x[0] * w for x, w in zip(parts, scales))
    total = sum(x[1] * w for x, w in zip(parts, scales))
    return num, total, peak


def kernel(
    rows, cols,
    rep_a, val_a, rep_b, val_b, back_a, back_b,
    in_a, in_b, values_t, scores, peak_a, peak_b,
    part_a, code_a, got_a, part_b, mate_b, code_b, got_b, done_a, done_b,
    own, cut_a_send, cut_b_send, a_recv, b_recv, a_send, b_send, mate_send,
    part_a_send, got_a_recv, mate_b_send, mate_b_recv, part_b_send, got_b_recv,
    done_a_send, done_b_send, done_a_recv, done_b_recv,
):
    Q, K = rows // HEADS, cols // 2
    n_a, n_b = rep_a.shape[0], rep_b.shape[0]
    row, col = lax.axis_index("row"), lax.axis_index("col")
    p, q = lax.div(row, Q), lax.rem(row, Q)
    k, c = lax.div(col, 2), lax.rem(col, 2)
    s = q * 2 + c
    to_log2 = HEAD ** -0.5 * math.log2(math.e)

    def head_at(d):
        return lax.rem(p + d, HEADS)

    def at_head(d):
        return (head_at(d) * Q + q, col)

    def at_k(d):
        return (row, lax.rem(k + d, K) * 2 + c)

    def at_q(d):
        return (p * Q + lax.rem(q + d, Q), col)

    mate = (row, k * 2 + 1 - c)

    def remote(src, dst, send, recv, device):
        return pltpu.make_async_remote_copy(
            src_ref=src, dst_ref=dst, send_sem=send, recv_sem=recv,
            device_id=device, device_id_type=MESH,
        )

    barrier = pltpu.get_barrier_semaphore()
    peers = [at_head(d) for d in range(1, HEADS)] + [at_k(d) for d in range(1, K)]
    peers += [at_q(d) for d in range(1, Q)] + [mate]
    for peer in peers:
        pl.semaphore_signal(barrier, inc=1, device_id=peer, device_id_type=MESH)

    def head_lanes(h):
        return pl.ds(pl.multiple_of(h * HEAD, HEAD), HEAD)

    own_lanes = head_lanes(p)
    own_copies = [
        pltpu.make_async_copy(x.at[:, own_lanes], y, own.at[i])
        for i, (x, y) in enumerate([
            (rep_b, in_b.at[s, p, 0]), (val_b, in_b.at[s, p, 1]),
            (rep_a, in_a.at[p, k, 0]), (val_a, in_a.at[p, k, 1]),
        ])
    ]
    for copy in own_copies:
        copy.start()
    peak_a[...] = jnp.full_like(peak_a, -jnp.inf)
    pl.semaphore_wait(barrier, len(peers))

    def cut_b_copy(d, i):
        return remote(
            (rep_b, val_b)[i].at[:, head_lanes(head_at(d))], in_b.at[s, p, i],
            cut_b_send.at[d, i], b_recv.at[s, p, i], at_head(d),
        )

    def cut_a_copy(d, i):
        return remote(
            (rep_a, val_a)[i].at[:, head_lanes(head_at(d))], in_a.at[p, k, i],
            cut_a_send.at[d, i], a_recv.at[k, p, i], at_head(d),
        )

    def a_copy(d, e, i):
        h = head_at(e)
        piece = in_a.at[h, k, i]
        return remote(piece, piece, a_send.at[d, e, i], a_recv.at[k, h, i], at_k(d))

    def b_copy(d, e, i):
        h = head_at(e)
        piece = in_b.at[s, h, i]
        return remote(piece, piece, b_send.at[d, e, i], b_recv.at[s, h, i], at_q(d))

    def mate_copy(d, e, i):
        r, h = lax.rem(q + d, Q) * 2 + c, head_at(e)
        piece = in_b.at[r, h, i]
        return remote(piece, piece, mate_send.at[d, e, i], b_recv.at[r, h, i], mate)

    def wait_b(r, e, i, device):
        h = head_at(e)
        piece = in_b.at[r, h, i]
        remote(piece, piece, mate_send.at[0, 0, i], b_recv.at[r, h, i], device).wait_recv()

    def wait_a(r, e, i, device):
        h = head_at(e)
        piece = in_a.at[h, r, i]
        remote(piece, piece, mate_send.at[0, 0, i], a_recv.at[r, h, i], device).wait_recv()

    def pass_b(e, i, own=False):
        if not own:
            wait_b(s, e, i, at_head(e))
        for d in range(1, Q):
            b_copy(d, e, i).start()
        mate_copy(0, e, i).start()

    def pass_b_to_mate(e, i):
        for d in range(1, Q):
            wait_b(lax.rem(q + d, Q) * 2 + c, e, i, at_q(d))
            mate_copy(d, e, i).start()

    def end_b(e, i):
        for d in range(Q):
            wait_b(lax.rem(q + d, Q) * 2 + 1 - c, e, i, mate)

    def pass_a(e, i, own=False):
        if not own:
            wait_a(k, e, i, at_head(e))
        for d in range(1, K):
            a_copy(d, e, i).start()

    def end_a(e, i):
        for d in range(1, K):
            wait_a(lax.rem(k + d, K), e, i, at_k(d))

    for cut, i in ((cut_a_copy, 0), (cut_b_copy, 0), (cut_a_copy, 1), (cut_b_copy, 1)):
        pl.loop(1, HEADS)(lambda d, cut=cut, i=i: cut(d, i).start())
    for copy in own_copies:
        copy.wait()
    for i in range(2):
        pass_a(0, i, own=True)
        pass_b(0, i, own=True)
    pl.loop(1, HEADS)(lambda e: pass_a(e, 0))

    @pl.loop(1, HEADS)
    def _(e):
        pass_b(e, 0)
        pass_b_to_mate(e - 1, 0)

    pl.loop(0, HEADS)(lambda e: end_a(e, 0))

    width = HEADS * n_b
    span = K * n_a
    def rows_at(e):
        return pl.ds(pl.multiple_of(head_at(e) * span, span), span)

    def lane_groups(x):
        return [x[:, j:j + HEAD] for j in range(0, width, HEAD)]

    def score_block(r):
        keys_t = in_b[r, :, 0].reshape(width, HEAD).T
        tops = jnp.full((8, width), -jnp.inf, jnp.float32)
        for h in range(HEADS):
            queries = in_a[h, :, 0].reshape(span, HEAD)
            logits = jnp.dot(queries, keys_t, preferred_element_type=jnp.float32) * to_log2
            scores[r, h * span:(h + 1) * span, :] = logits
            tops = jnp.maximum(tops, jnp.max(logits.reshape(span // 8, 8, width), axis=0))
            peak_a[h] = functools.reduce(jnp.maximum, lane_groups(logits), peak_a[h])
        peak_b[r] = tops

    @pl.loop(0, 2 * Q)
    def _(t):
        @pl.when(t == 1)
        def _():
            pass_b_to_mate(HEADS - 1, 0)

        near = t < Q
        r = lax.rem(q + lax.rem(t, Q), Q) * 2 + jnp.where(near, c, 1 - c)

        @pl.when(t >= Q)
        def _():
            pl.loop(0, HEADS)(lambda e: wait_b(r, e, 0, mate))

        score_block(r)

        @pl.when((t > 0) & (t < HEADS))
        def _():
            pass_a(t, 1)

    for e in range(2 * Q, HEADS):
        pass_a(e, 1)

    def row_block(e):
        pp = head_at(e)
        peak = jnp.max(peak_a[pp], axis=1, keepdims=True)
        totals = jnp.zeros((span, HEAD), jnp.float32)
        num = jnp.zeros((span, HEAD), jnp.float32)
        for r in range(2 * Q):
            values = in_b[r, :, 1].reshape(width, HEAD)
            weights = jnp.exp2(scores[r, rows_at(e), :] - peak)
            totals = functools.reduce(jnp.add, lane_groups(weights), totals)
            num += jnp.dot(
                weights.astype(jnp.bfloat16), values, preferred_element_type=jnp.float32
            )
        total = jnp.sum(totals, axis=1, keepdims=True)
        lane = lax.broadcasted_iota(jnp.int32, (span, HEAD), 1)
        stats = jnp.where(lane == 0, peak, total)
        for kk in range(K):
            mine = slice(kk * n_a, (kk + 1) * n_a)
            num_t = num[mine].T
            stats_t = stats[mine].T[0:STATS]
            part_a[kk, pp, 0:HEAD] = num_t
            part_a[kk, pp, HEAD:HEAD + STATS] = stats_t
            codes, extra = packed_part(num_t, stats_t[1:2], stats_t[0:1])
            code_a[kk, pp, 0:HEAD] = codes
            code_a[kk, pp, HEAD:HEAD + EXTRA] = extra

    def part_a_copy(d, e):
        there = lax.rem(k + d, K)
        h = head_at(e)
        return remote(
            code_a.at[there, h], got_a.at[k, h], part_a_send.at[d, e], got_a_recv.at[k, h], at_k(d)
        )

    pl.loop(0, HEADS)(lambda e: end_a(e, 1))
    values_t[...] = in_a[:, :, 1].reshape(HEADS * span, HEAD).T

    def col_block(r):
        peak = jnp.max(peak_b[r], axis=0, keepdims=True)
        weights = jnp.exp2(scores[r] - peak)
        total = jnp.sum(weights, axis=0, keepdims=True)
        num = jnp.dot(values_t[...], weights.astype(jnp.bfloat16), preferred_element_type=jnp.float32)
        sub = lax.broadcasted_iota(jnp.int32, (STATS, width), 0)
        stats = jnp.where(sub == 0, peak, total)
        for h in range(HEADS):
            part_b[r, h, 0:HEAD] = num[:, h * n_b:(h + 1) * n_b]
            part_b[r, h, HEAD:HEAD + STATS] = stats[:, h * n_b:(h + 1) * n_b]

    def mate_b_copy(d):
        qq = lax.rem(q + d, Q)
        return remote(
            part_b.at[qq * 2 + 1 - c], mate_b.at[qq], mate_b_send.at[d], mate_b_recv.at[qq], mate
        )

    def part_b_copy(d, e):
        h = head_at(e)
        return remote(
            code_b.at[lax.rem(q + d, Q), h], got_b.at[q, h], part_b_send.at[d, e], got_b_recv.at[q, h], at_q(d)
        )

    def part_of(ref):
        return ref[0:HEAD], ref[HEAD + 1:HEAD + 2], ref[HEAD:HEAD + 1]

    def sent_part_of(ref):
        return unpacked_part(ref[0:HEAD], ref[HEAD:HEAD + EXTRA])

    def done_copy(e, done, back, send, recv):
        return remote(done.at[head_at(e)], back.at[p], send.at[e], recv.at[p], at_head(e))

    def wait_done(e, done, back, send, recv):
        h = head_at(e)
        remote(done.at[h], back.at[h], send.at[e], recv.at[h], at_head(e)).wait_recv()

    def finish(e, parts, done, back, send, recv):
        num, total, _ = merged(parts)
        result = (num / total).T
        n = result.shape[0]
        scale = scale_of(result)
        codes = code_of(result, scale.astype(jnp.float32))
        extra = jnp.broadcast_to(scale, (EXTRA, HEAD))

        @pl.when(e > 0)
        def _():
            done[head_at(e), 0:n] = codes
            done[head_at(e), n:n + EXTRA] = extra
            done_copy(e, done, back, send, recv).start()

        @pl.when(e == 0)
        def _():
            back[p, 0:n] = codes
            back[p, n:n + EXTRA] = extra

    def finish_a(e):
        h = head_at(e)
        parts = [part_of(part_a.at[k, h])]
        for d in range(1, K):
            kk = lax.rem(k + d, K)
            remote(
                code_a.at[kk, h], got_a.at[kk, h], part_a_send.at[d, e], got_a_recv.at[kk, h],
                at_k(d),
            ).wait_recv()
            parts.append(sent_part_of(got_a.at[kk, h]))
        finish(e, parts, done_a, back_a, done_a_send, done_a_recv)

    def finish_b(e):
        h = head_at(e)
        parts = [part_of(part_b.at[s, h])]
        for d in range(1, Q):
            qq = lax.rem(q + d, Q)
            remote(
                code_b.at[qq, h], got_b.at[qq, h], part_b_send.at[d, e],
                got_b_recv.at[qq, h], at_q(d),
            ).wait_recv()
            parts.append(sent_part_of(got_b.at[qq, h]))
        finish(e, parts, done_b, back_b, done_b_send, done_b_recv)

    def merge_mate(d):
        qq = lax.rem(q + d, Q)
        mate_b_copy(d).wait_recv()

        @pl.loop(0, HEADS)
        def _(e):
            h = head_at(e)
            both = merged([part_of(part_b.at[qq * 2 + c, h]), part_of(mate_b.at[qq, h])])

            @pl.when(d > 0)
            def _():
                codes, extra = packed_part(*both)
                code_b[qq, h, 0:HEAD] = codes
                code_b[qq, h, HEAD:HEAD + EXTRA] = extra
                part_b_copy(d, e).start()

            @pl.when(d == 0)
            def _():
                part_b[qq * 2 + c, h, 0:HEAD] = both[0]
                part_b[qq * 2 + c, h, HEAD:HEAD + 1] = both[2]
                part_b[qq * 2 + c, h, HEAD + 1:HEAD + 2] = both[1]

    @pl.loop(0, 2 * Q)
    def _(t):
        d = lax.rem(t + 1, Q)
        first = t < Q
        col_block(lax.rem(q + d, Q) * 2 + jnp.where(first, 1 - c, c))

        @pl.when(first)
        def _():
            mate_b_copy(d).start()

        @pl.when(t == 0)
        def _():
            pl.loop(1, HEADS)(lambda e: pass_b(e, 1))

        @pl.when(t == Q - 1)
        def _():
            pl.loop(0, HEADS)(lambda e: pass_b_to_mate(e, 1))

        @pl.when(t >= Q)
        def _():
            merge_mate(d)

    pl.loop(0, HEADS)(lambda e: end_b(e, 1))

    @pl.loop(0, HEADS + 1)
    def _(n):
        @pl.when(n < HEADS)
        def _():
            e = lax.rem(n + 1, HEADS)
            row_block(e)
            for d in range(1, K):
                part_a_copy(d, e).start()
            finish_b(e)

        @pl.when(n > 0)
        def _():
            finish_a(lax.rem(n, HEADS))

    @pl.loop(1, HEADS)
    def _(e):
        wait_done(e, done_b, back_b, done_b_send, done_b_recv)
        wait_done(e, done_a, back_a, done_a_send, done_a_recv)

    @pl.loop(1, HEADS)
    def _(e):
        for i in range(2):
            cut_b_copy(e, i).wait_send()
            cut_a_copy(e, i).wait_send()
        done_copy(e, done_a, back_a, done_a_send, done_a_recv).wait_send()
        done_copy(e, done_b, back_b, done_b_send, done_b_recv).wait_send()

    @pl.loop(0, HEADS)
    def _(e):
        for d in range(1, K):
            for i in range(2):
                a_copy(d, e, i).wait_send()
            part_a_copy(d, e).wait_send()
        for d in range(Q):
            for i in range(2):
                if d:
                    b_copy(d, e, i).wait_send()
                mate_copy(d, e, i).wait_send()
            if d:
                part_b_copy(d, e).wait_send()

    pl.loop(0, Q)(lambda d: mate_b_copy(d).wait_send())


def decode(back_a, back_b, out_a, out_b):
    for back, out in ((back_a, out_a), (back_b, out_b)):
        n = out.shape[0]
        for h in range(HEADS):
            scale = back[h, n:n + EXTRA].astype(jnp.float32)[0:1]
            out[:, h * HEAD:(h + 1) * HEAD] = value_of(back[h, 0:n], scale)


def on_device(rows, cols, rep_a, val_a, rep_b, val_b):
    Q, K = rows // HEADS, cols // 2
    n_a, n_b = rep_a.shape[0], rep_b.shape[0]
    f32, bf16 = jnp.float32, jnp.bfloat16
    tall = HEAD + STATS
    dma = pltpu.SemaphoreType.DMA
    vmem = pl.BlockSpec(memory_space=pltpu.VMEM)
    hbm = pl.BlockSpec(memory_space=pltpu.HBM)
    tile = K * HEADS * n_a * 2 * Q * HEADS * n_b
    back_a, back_b = pl.pallas_call(
        functools.partial(kernel, rows, cols),
        out_shape=(
            jax.ShapeDtypeStruct((HEADS, n_a + EXTRA, HEAD), bf16),
            jax.ShapeDtypeStruct((HEADS, n_b + EXTRA, HEAD), bf16),
        ),
        in_specs=[hbm] * 4,
        out_specs=(vmem, vmem),
        scratch_shapes=[
            pltpu.VMEM((HEADS, K, 2, n_a, HEAD), bf16),
            pltpu.VMEM((2 * Q, HEADS, 2, n_b, HEAD), bf16),
            pltpu.VMEM((HEAD, HEADS * K * n_a), bf16),
            pltpu.VMEM((2 * Q, K * HEADS * n_a, HEADS * n_b), f32),
            pltpu.VMEM((HEADS, K * n_a, HEAD), f32),
            pltpu.VMEM((2 * Q, 8, HEADS * n_b), f32),
            pltpu.VMEM((K, HEADS, tall, n_a), f32),
            pltpu.VMEM((K, HEADS, HEAD + EXTRA, n_a), bf16),
            pltpu.VMEM((K, HEADS, HEAD + EXTRA, n_a), bf16),
            pltpu.VMEM((2 * Q, HEADS, tall, n_b), f32),
            pltpu.VMEM((Q, HEADS, tall, n_b), f32),
            pltpu.VMEM((Q, HEADS, HEAD + EXTRA, n_b), bf16),
            pltpu.VMEM((Q, HEADS, HEAD + EXTRA, n_b), bf16),
            pltpu.VMEM((HEADS, n_a + EXTRA, HEAD), bf16),
            pltpu.VMEM((HEADS, n_b + EXTRA, HEAD), bf16),
            dma((4,)), dma((HEADS, 2)), dma((HEADS, 2)),
            dma((K, HEADS, 2)), dma((2 * Q, HEADS, 2)),
            dma((K, HEADS, 2)), dma((Q, HEADS, 2)), dma((Q, HEADS, 2)),
            dma((K, HEADS)), dma((K, HEADS)),
            dma((Q,)), dma((Q,)),
            dma((Q, HEADS)), dma((Q, HEADS)),
            dma((HEADS,)), dma((HEADS,)), dma((HEADS,)), dma((HEADS,)),
        ],
        compiler_params=pltpu.CompilerParams(
            collective_id=0, has_side_effects=True, vmem_limit_bytes=GRANT
        ),
        cost_estimate=pl.CostEstimate(
            flops=6 * tile * HEAD, bytes_accessed=6 * 1024 * (n_a + n_b), transcendentals=2 * tile
        ),
    )(rep_a, val_a, rep_b, val_b)
    return pl.pallas_call(
        decode,
        out_shape=(
            jax.ShapeDtypeStruct(rep_a.shape, f32),
            jax.ShapeDtypeStruct(rep_b.shape, f32),
        ),
        in_specs=[vmem] * 2,
        out_specs=(vmem, vmem),
        compiler_params=pltpu.CompilerParams(vmem_limit_bytes=GRANT),
    )(back_a, back_b)


def solution(mesh):
    rows, cols = mesh.shape["row"], mesh.shape["col"]
    placed = P(("row", "col"), None)
    return jax.shard_map(
        functools.partial(on_device, rows, cols),
        mesh=mesh,
        in_specs=(placed,) * 4,
        out_specs=(placed, placed),
        check_vma=False,
    )
```

```python
import functools
import math

import jax
import jax.numpy as jnp
from jax import lax
from jax.experimental import pallas as pl
from jax.experimental.pallas import tpu as pltpu
from jax.sharding import PartitionSpec as P

HEADS = 4
HEAD = 128
STATS = 8
EXTRA = 16
BINADES = 248.0
GRANT = 127 * 512 * 1024
MESH = pl.DeviceIdType.MESH


def code_of(x, scale):
    code = jnp.exp2(jnp.abs(x) * (BINADES / scale) - BINADES / 2)
    return jnp.where(x < 0, -code, code).astype(jnp.bfloat16)


def value_of(code, scale):
    code = code.astype(jnp.float32)
    size = jnp.log(jnp.abs(code)) * (1 / (math.log(2) * BINADES)) + 0.5
    return jnp.where(code < 0, -size, size) * scale


def scale_of(x):
    largest = jnp.max(jnp.abs(x), axis=0, keepdims=True) * 1.01 + 1e-30
    return largest.astype(jnp.bfloat16)


def three_terms(x):
    terms = []
    for _ in range(3):
        term = x.astype(jnp.bfloat16).astype(jnp.float32)
        terms.append(term)
        x = x - term
    return terms


def packed_part(num, total, peak):
    mean = num / total
    scale = scale_of(mean).astype(jnp.float32)
    rows = [scale] + three_terms(peak) + three_terms(total)
    sub = lax.broadcasted_iota(jnp.int32, (EXTRA, num.shape[1]), 0)
    extra = jnp.zeros((EXTRA, num.shape[1]), jnp.float32)
    for i, x in enumerate(rows):
        extra = jnp.where(sub == i, x, extra)
    return code_of(mean, scale), extra.astype(jnp.bfloat16)


def unpacked_part(codes, extra):
    extra = extra.astype(jnp.float32)
    peak = extra[1:2] + extra[2:3] + extra[3:4]
    total = extra[4:5] + extra[5:6] + extra[6:7]
    return value_of(codes, extra[0:1]) * total, total, peak


def merged(parts):
    peak = functools.reduce(jnp.maximum, [x[2] for x in parts])
    scales = [jnp.exp2(x[2] - peak) for x in parts]
    num = sum(x[0] * w for x, w in zip(parts, scales))
    total = sum(x[1] * w for x, w in zip(parts, scales))
    return num, total, peak


def kernel(
    rows, cols,
    rep_a, val_a, rep_b, val_b, back_a, back_b,
    in_a, in_b, values_t, scores, peak_a, peak_b,
    part_a, code_a, got_a, part_b, mate_b, code_b, got_b, done_a, done_b,
    own, cut_a_send, cut_b_send, a_recv, b_recv, a_all, b_all, a_send, b_send, mate_send,
    part_a_send, got_a_recv, mate_b_send, mate_b_recv, part_b_send, got_b_recv,
    done_a_send, done_b_send, done_a_recv, done_b_recv,
):
    Q, K = rows // HEADS, cols // 2
    n_a, n_b = rep_a.shape[0], rep_b.shape[0]
    row, col = lax.axis_index("row"), lax.axis_index("col")
    p, q = lax.div(row, Q), lax.rem(row, Q)
    k, c = lax.div(col, 2), lax.rem(col, 2)
    s = q * 2 + c
    to_log2 = HEAD ** -0.5 * math.log2(math.e)

    def head_at(d):
        return lax.rem(p + d, HEADS)

    def at_head(d):
        return (head_at(d) * Q + q, col)

    def at_k(d):
        return (row, lax.rem(k + d, K) * 2 + c)

    def at_q(d):
        return (p * Q + lax.rem(q + d, Q), col)

    mate = (row, k * 2 + 1 - c)

    def remote(src, dst, send, recv, device):
        return pltpu.make_async_remote_copy(
            src_ref=src, dst_ref=dst, send_sem=send, recv_sem=recv,
            device_id=device, device_id_type=MESH,
        )

    barrier = pltpu.get_barrier_semaphore()
    peers = [at_head(d) for d in range(1, HEADS)] + [at_k(d) for d in range(1, K)]
    peers += [at_q(d) for d in range(1, Q)] + [mate]
    for peer in peers:
        pl.semaphore_signal(barrier, inc=1, device_id=peer, device_id_type=MESH)

    def head_lanes(h):
        return pl.ds(pl.multiple_of(h * HEAD, HEAD), HEAD)

    own_lanes = head_lanes(p)
    own_copies = [
        pltpu.make_async_copy(x.at[:, own_lanes], y, own.at[i])
        for i, (x, y) in enumerate([
            (rep_b, in_b.at[s, p, 0]), (val_b, in_b.at[s, p, 1]),
            (rep_a, in_a.at[p, k, 0]), (val_a, in_a.at[p, k, 1]),
        ])
    ]
    for copy in own_copies:
        copy.start()
    peak_a[...] = jnp.full_like(peak_a, -jnp.inf)
    pl.semaphore_wait(barrier, len(peers))

    def cut_b_copy(d, i):
        return remote(
            (rep_b, val_b)[i].at[:, head_lanes(head_at(d))], in_b.at[s, p, i],
            cut_b_send.at[d, i], b_recv.at[s, p, i], at_head(d),
        )

    def cut_a_copy(d, i):
        return remote(
            (rep_a, val_a)[i].at[:, head_lanes(head_at(d))], in_a.at[p, k, i],
            cut_a_send.at[d, i], a_recv.at[k, p, i], at_head(d),
        )

    def a_copy(d, e, i):
        piece = in_a.at[head_at(e), k, i]
        return remote(piece, piece, a_send.at[d, e, i], a_all.at[k, i], at_k(d))

    def b_copy(d, e, i):
        piece = in_b.at[s, head_at(e), i]
        return remote(piece, piece, b_send.at[d, e, i], b_all.at[s, i], at_q(d))

    def mate_copy(d, i):
        r = lax.rem(q + d, Q) * 2 + c
        block = in_b.at[r, :, i]
        return remote(block, block, mate_send.at[d, i], b_all.at[r, i], mate)

    def pass_b(e, i, own=False):
        if not own:
            piece = in_b.at[s, head_at(e), i]
            remote(
                piece, piece, cut_b_send.at[e, i], b_recv.at[s, head_at(e), i], at_head(e)
            ).wait_recv()
        for d in range(1, Q):
            b_copy(d, e, i).start()

    def wait_b(r, i, device):
        block = in_b.at[r, :, i]
        remote(block, block, mate_send.at[0, i], b_all.at[r, i], device).wait_recv()

    def pass_b_to_mate(i):
        for d in range(1, Q):
            wait_b(lax.rem(q + d, Q) * 2 + c, i, at_q(d))
            mate_copy(d, i).start()

    def pass_a(e, i, own=False):
        if not own:
            piece = in_a.at[head_at(e), k, i]
            remote(
                piece, piece, cut_a_send.at[e, i], a_recv.at[k, head_at(e), i], at_head(e)
            ).wait_recv()
        for d in range(1, K):
            a_copy(d, e, i).start()

    def end_a(i):
        for d in range(1, K):
            block = in_a.at[:, lax.rem(k + d, K), i]
            remote(
                block, block, a_send.at[d, 0, i], a_all.at[lax.rem(k + d, K), i], at_k(d)
            ).wait_recv()

    for cut, i in ((cut_a_copy, 0), (cut_b_copy, 0), (cut_a_copy, 1), (cut_b_copy, 1)):
        pl.loop(1, HEADS)(lambda d, cut=cut, i=i: cut(d, i).start())
    for copy in own_copies:
        copy.wait()
    for i in range(2):
        pass_a(0, i, own=True)
        pass_b(0, i, own=True)
    pl.loop(1, HEADS)(lambda e: pass_a(e, 0))

    pl.loop(1, HEADS)(lambda e: pass_b(e, 0))
    mate_copy(0, 0).start()
    end_a(0)

    width = HEADS * n_b
    span = K * n_a
    def rows_at(e):
        return pl.ds(pl.multiple_of(head_at(e) * span, span), span)

    def lane_groups(x):
        return [x[:, j:j + HEAD] for j in range(0, width, HEAD)]

    def score_block(r):
        keys_t = in_b[r, :, 0].reshape(width, HEAD).T
        tops = jnp.full((8, width), -jnp.inf, jnp.float32)
        for h in range(HEADS):
            queries = in_a[h, :, 0].reshape(span, HEAD)
            logits = jnp.dot(queries, keys_t, preferred_element_type=jnp.float32) * to_log2
            scores[r, h * span:(h + 1) * span, :] = logits
            tops = jnp.maximum(tops, jnp.max(logits.reshape(span // 8, 8, width), axis=0))
            peak_a[h] = functools.reduce(jnp.maximum, lane_groups(logits), peak_a[h])
        peak_b[r] = tops

    @pl.loop(0, 2 * Q)
    def _(t):
        @pl.when(t == 1)
        def _():
            pass_b_to_mate(0)

        near = t < Q
        r = lax.rem(q + lax.rem(t, Q), Q) * 2 + jnp.where(near, c, 1 - c)

        @pl.when(t >= Q)
        def _():
            wait_b(r, 0, mate)

        score_block(r)

        @pl.when((t > 0) & (t < HEADS))
        def _():
            pass_a(t, 1)

    for e in range(2 * Q, HEADS):
        pass_a(e, 1)

    def row_block(e):
        pp = head_at(e)
        peak = jnp.max(peak_a[pp], axis=1, keepdims=True)
        totals = jnp.zeros((span, HEAD), jnp.float32)
        num = jnp.zeros((span, HEAD), jnp.float32)
        for r in range(2 * Q):
            values = in_b[r, :, 1].reshape(width, HEAD)
            weights = jnp.exp2(scores[r, rows_at(e), :] - peak)
            totals = functools.reduce(jnp.add, lane_groups(weights), totals)
            num += jnp.dot(
                weights.astype(jnp.bfloat16), values, preferred_element_type=jnp.float32
            )
        total = jnp.sum(totals, axis=1, keepdims=True)
        lane = lax.broadcasted_iota(jnp.int32, (span, HEAD), 1)
        stats = jnp.where(lane == 0, peak, total)
        for kk in range(K):
            mine = slice(kk * n_a, (kk + 1) * n_a)
            num_t = num[mine].T
            stats_t = stats[mine].T[0:STATS]
            part_a[kk, pp, 0:HEAD] = num_t
            part_a[kk, pp, HEAD:HEAD + STATS] = stats_t
            codes, extra = packed_part(num_t, stats_t[1:2], stats_t[0:1])
            code_a[kk, pp, 0:HEAD] = codes
            code_a[kk, pp, HEAD:HEAD + EXTRA] = extra

    def part_a_copy(d, e):
        there = lax.rem(k + d, K)
        h = head_at(e)
        return remote(
            code_a.at[there, h], got_a.at[k, h], part_a_send.at[d, e], got_a_recv.at[k, h], at_k(d)
        )

    end_a(1)
    values_t[...] = in_a[:, :, 1].reshape(HEADS * span, HEAD).T

    def col_block(r):
        peak = jnp.max(peak_b[r], axis=0, keepdims=True)
        weights = jnp.exp2(scores[r] - peak)
        total = jnp.sum(weights, axis=0, keepdims=True)
        num = jnp.dot(values_t[...], weights.astype(jnp.bfloat16), preferred_element_type=jnp.float32)
        sub = lax.broadcasted_iota(jnp.int32, (STATS, width), 0)
        stats = jnp.where(sub == 0, peak, total)
        for h in range(HEADS):
            part_b[r, h, 0:HEAD] = num[:, h * n_b:(h + 1) * n_b]
            part_b[r, h, HEAD:HEAD + STATS] = stats[:, h * n_b:(h + 1) * n_b]

    def mate_b_copy(d):
        qq = lax.rem(q + d, Q)
        return remote(
            part_b.at[qq * 2 + 1 - c], mate_b.at[qq], mate_b_send.at[d], mate_b_recv.at[qq], mate
        )

    def part_b_copy(d, e):
        h = head_at(e)
        return remote(
            code_b.at[lax.rem(q + d, Q), h], got_b.at[q, h], part_b_send.at[d, e], got_b_recv.at[q, h], at_q(d)
        )

    def part_of(ref):
        return ref[0:HEAD], ref[HEAD + 1:HEAD + 2], ref[HEAD:HEAD + 1]

    def sent_part_of(ref):
        return unpacked_part(ref[0:HEAD], ref[HEAD:HEAD + EXTRA])

    def done_copy(e, done, back, send, recv):
        return remote(done.at[head_at(e)], back.at[p], send.at[e], recv.at[p], at_head(e))

    def wait_done(e, done, back, send, recv):
        h = head_at(e)
        remote(done.at[h], back.at[h], send.at[e], recv.at[h], at_head(e)).wait_recv()

    def finish(e, parts, done, back, send, recv):
        num, total, _ = merged(parts)
        result = (num / total).T
        n = result.shape[0]
        scale = scale_of(result)
        codes = code_of(result, scale.astype(jnp.float32))
        extra = jnp.broadcast_to(scale, (EXTRA, HEAD))

        @pl.when(e > 0)
        def _():
            done[head_at(e), 0:n] = codes
            done[head_at(e), n:n + EXTRA] = extra
            done_copy(e, done, back, send, recv).start()

        @pl.when(e == 0)
        def _():
            back[p, 0:n] = codes
            back[p, n:n + EXTRA] = extra

    def finish_a(e):
        h = head_at(e)
        parts = [part_of(part_a.at[k, h])]
        for d in range(1, K):
            kk = lax.rem(k + d, K)
            remote(
                code_a.at[kk, h], got_a.at[kk, h], part_a_send.at[d, e], got_a_recv.at[kk, h],
                at_k(d),
            ).wait_recv()
            parts.append(sent_part_of(got_a.at[kk, h]))
        finish(e, parts, done_a, back_a, done_a_send, done_a_recv)

    def finish_b(e):
        h = head_at(e)
        parts = [part_of(part_b.at[s, h])]
        for d in range(1, Q):
            qq = lax.rem(q + d, Q)
            remote(
                code_b.at[qq, h], got_b.at[qq, h], part_b_send.at[d, e],
                got_b_recv.at[qq, h], at_q(d),
            ).wait_recv()
            parts.append(sent_part_of(got_b.at[qq, h]))
        finish(e, parts, done_b, back_b, done_b_send, done_b_recv)

    def merge_mate(d):
        qq = lax.rem(q + d, Q)
        mate_b_copy(d).wait_recv()

        @pl.loop(0, HEADS)
        def _(e):
            h = head_at(e)
            both = merged([part_of(part_b.at[qq * 2 + c, h]), part_of(mate_b.at[qq, h])])

            @pl.when(d > 0)
            def _():
                codes, extra = packed_part(*both)
                code_b[qq, h, 0:HEAD] = codes
                code_b[qq, h, HEAD:HEAD + EXTRA] = extra
                part_b_copy(d, e).start()

            @pl.when(d == 0)
            def _():
                part_b[qq * 2 + c, h, 0:HEAD] = both[0]
                part_b[qq * 2 + c, h, HEAD:HEAD + 1] = both[2]
                part_b[qq * 2 + c, h, HEAD + 1:HEAD + 2] = both[1]

    @pl.loop(0, 2 * Q)
    def _(t):
        d = lax.rem(t + 1, Q)
        first = t < Q
        col_block(lax.rem(q + d, Q) * 2 + jnp.where(first, 1 - c, c))

        @pl.when(first)
        def _():
            mate_b_copy(d).start()

        @pl.when(t == 0)
        def _():
            pl.loop(1, HEADS)(lambda e: pass_b(e, 1))
            mate_copy(0, 1).start()

        @pl.when(t == Q - 1)
        def _():
            pass_b_to_mate(1)

        @pl.when(t >= Q)
        def _():
            merge_mate(d)

    for d in range(Q):
        wait_b(lax.rem(q + d, Q) * 2 + 1 - c, 1, mate)

    @pl.loop(0, HEADS + 1)
    def _(n):
        @pl.when(n < HEADS)
        def _():
            e = lax.rem(n + 1, HEADS)
            row_block(e)
            for d in range(1, K):
                part_a_copy(d, e).start()

        @pl.when(n > 0)
        def _():
            finish_b(lax.rem(n, HEADS))
            finish_a(lax.rem(n, HEADS))

    @pl.loop(1, HEADS)
    def _(e):
        for i in range(2):
            cut_b_copy(e, i).wait_send()
            cut_a_copy(e, i).wait_send()

    @pl.loop(0, HEADS)
    def _(e):
        for d in range(1, K):
            for i in range(2):
                a_copy(d, e, i).wait_send()
            part_a_copy(d, e).wait_send()
        for d in range(1, Q):
            for i in range(2):
                b_copy(d, e, i).wait_send()
            part_b_copy(d, e).wait_send()

    for d in range(Q):
        for i in range(2):
            mate_copy(d, i).wait_send()
        mate_b_copy(d).wait_send()

    @pl.loop(1, HEADS)
    def _(e):
        done_copy(e, done_a, back_a, done_a_send, done_a_recv).wait_send()
        done_copy(e, done_b, back_b, done_b_send, done_b_recv).wait_send()
        wait_done(e, done_b, back_b, done_b_send, done_b_recv)
        wait_done(e, done_a, back_a, done_a_send, done_a_recv)


def decode(back_a, back_b, out_a, out_b):
    for back, out in ((back_a, out_a), (back_b, out_b)):
        n = out.shape[0]
        for h in range(HEADS):
            scale = back[h, n:n + EXTRA].astype(jnp.float32)[0:1]
            out[:, h * HEAD:(h + 1) * HEAD] = value_of(back[h, 0:n], scale)


def on_device(rows, cols, rep_a, val_a, rep_b, val_b):
    Q, K = rows // HEADS, cols // 2
    n_a, n_b = rep_a.shape[0], rep_b.shape[0]
    f32, bf16 = jnp.float32, jnp.bfloat16
    tall = HEAD + STATS
    dma = pltpu.SemaphoreType.DMA
    vmem = pl.BlockSpec(memory_space=pltpu.VMEM)
    hbm = pl.BlockSpec(memory_space=pltpu.HBM)
    tile = K * HEADS * n_a * 2 * Q * HEADS * n_b
    back_a, back_b = pl.pallas_call(
        functools.partial(kernel, rows, cols),
        out_shape=(
            jax.ShapeDtypeStruct((HEADS, n_a + EXTRA, HEAD), bf16),
            jax.ShapeDtypeStruct((HEADS, n_b + EXTRA, HEAD), bf16),
        ),
        in_specs=[hbm] * 4,
        out_specs=(vmem, vmem),
        scratch_shapes=[
            pltpu.VMEM((HEADS, K, 2, n_a, HEAD), bf16),
            pltpu.VMEM((2 * Q, HEADS, 2, n_b, HEAD), bf16),
            pltpu.VMEM((HEAD, HEADS * K * n_a), bf16),
            pltpu.VMEM((2 * Q, K * HEADS * n_a, HEADS * n_b), f32),
            pltpu.VMEM((HEADS, K * n_a, HEAD), f32),
            pltpu.VMEM((2 * Q, 8, HEADS * n_b), f32),
            pltpu.VMEM((K, HEADS, tall, n_a), f32),
            pltpu.VMEM((K, HEADS, HEAD + EXTRA, n_a), bf16),
            pltpu.VMEM((K, HEADS, HEAD + EXTRA, n_a), bf16),
            pltpu.VMEM((2 * Q, HEADS, tall, n_b), f32),
            pltpu.VMEM((Q, HEADS, tall, n_b), f32),
            pltpu.VMEM((Q, HEADS, HEAD + EXTRA, n_b), bf16),
            pltpu.VMEM((Q, HEADS, HEAD + EXTRA, n_b), bf16),
            pltpu.VMEM((HEADS, n_a + EXTRA, HEAD), bf16),
            pltpu.VMEM((HEADS, n_b + EXTRA, HEAD), bf16),
            dma((4,)), dma((HEADS, 2)), dma((HEADS, 2)),
            dma((K, HEADS, 2)), dma((2 * Q, HEADS, 2)),
            dma((K, 2)), dma((2 * Q, 2)),
            dma((K, HEADS, 2)), dma((Q, HEADS, 2)), dma((Q, 2)),
            dma((K, HEADS)), dma((K, HEADS)),
            dma((Q,)), dma((Q,)),
            dma((Q, HEADS)), dma((Q, HEADS)),
            dma((HEADS,)), dma((HEADS,)), dma((HEADS,)), dma((HEADS,)),
        ],
        compiler_params=pltpu.CompilerParams(
            collective_id=0, has_side_effects=True, vmem_limit_bytes=GRANT
        ),
        cost_estimate=pl.CostEstimate(
            flops=6 * tile * HEAD, bytes_accessed=6 * 1024 * (n_a + n_b), transcendentals=2 * tile
        ),
    )(rep_a, val_a, rep_b, val_b)
    return pl.pallas_call(
        decode,
        out_shape=(
            jax.ShapeDtypeStruct(rep_a.shape, f32),
            jax.ShapeDtypeStruct(rep_b.shape, f32),
        ),
        in_specs=[vmem] * 2,
        out_specs=(vmem, vmem),
        compiler_params=pltpu.CompilerParams(vmem_limit_bytes=GRANT),
    )(back_a, back_b)


def solution(mesh):
    rows, cols = mesh.shape["row"], mesh.shape["col"]
    placed = P(("row", "col"), None)
    return jax.shard_map(
        functools.partial(on_device, rows, cols),
        mesh=mesh,
        in_specs=(placed,) * 4,
        out_specs=(placed, placed),
        check_vma=False,
    )
```

```python
import functools
import math

import jax
import jax.numpy as jnp
from jax import lax
from jax.experimental import pallas as pl
from jax.experimental.pallas import tpu as pltpu
from jax.sharding import PartitionSpec as P

HEADS = 4
HEAD = 128
STATS = 8
EXTRA = 16
BINADES = 248.0
GRANT = 127 * 512 * 1024
MESH = pl.DeviceIdType.MESH


def code_of(x, scale):
    code = jnp.exp2(jnp.abs(x) * (BINADES / scale) - BINADES / 2)
    return jnp.where(x < 0, -code, code).astype(jnp.bfloat16)


def value_of(code, scale):
    code = code.astype(jnp.float32)
    size = jnp.log(jnp.abs(code)) * (1 / (math.log(2) * BINADES)) + 0.5
    return jnp.where(code < 0, -size, size) * scale


def scale_of(x):
    largest = jnp.max(jnp.abs(x), axis=0, keepdims=True) * 1.01 + 1e-30
    return largest.astype(jnp.bfloat16)


def three_terms(x):
    terms = []
    for _ in range(3):
        term = x.astype(jnp.bfloat16).astype(jnp.float32)
        terms.append(term)
        x = x - term
    return terms


def packed_part(num, total, peak):
    mean = num / total
    scale = scale_of(mean).astype(jnp.float32)
    rows = [scale] + three_terms(peak) + three_terms(total)
    sub = lax.broadcasted_iota(jnp.int32, (EXTRA, num.shape[1]), 0)
    extra = jnp.zeros((EXTRA, num.shape[1]), jnp.float32)
    for i, x in enumerate(rows):
        extra = jnp.where(sub == i, x, extra)
    return code_of(mean, scale), extra.astype(jnp.bfloat16)


def unpacked_part(codes, extra):
    extra = extra.astype(jnp.float32)
    peak = extra[1:2] + extra[2:3] + extra[3:4]
    total = extra[4:5] + extra[5:6] + extra[6:7]
    return value_of(codes, extra[0:1]) * total, total, peak


def merged(parts):
    peak = functools.reduce(jnp.maximum, [x[2] for x in parts])
    scales = [jnp.exp2(x[2] - peak) for x in parts]
    num = sum(x[0] * w for x, w in zip(parts, scales))
    total = sum(x[1] * w for x, w in zip(parts, scales))
    return num, total, peak


def kernel(
    rows, cols,
    rep_a, val_a, rep_b, val_b, back_a, back_b,
    in_a, in_b, values_t, scores, peak_a, peak_b,
    part_a, code_a, got_a, part_b, mate_b, code_b, got_b, done_a, done_b,
    own, cut_a_send, cut_b_send, a_recv, b_recv, a_all, b_all, a_send, b_send, mate_send,
    part_a_send, got_a_recv, mate_b_send, mate_b_recv, part_b_send, got_b_recv,
    done_a_send, done_b_send, done_a_recv, done_b_recv,
):
    Q, K = rows // HEADS, cols // 2
    n_a, n_b = rep_a.shape[0], rep_b.shape[0]
    row, col = lax.axis_index("row"), lax.axis_index("col")
    p, q = lax.div(row, Q), lax.rem(row, Q)
    k, c = lax.div(col, 2), lax.rem(col, 2)
    s = q * 2 + c
    to_log2 = HEAD ** -0.5 * math.log2(math.e)

    def head_at(d):
        return lax.rem(p + d, HEADS)

    def at_head(d):
        return (head_at(d) * Q + q, col)

    def at_k(d):
        return (row, lax.rem(k + d, K) * 2 + c)

    def at_q(d):
        return (p * Q + lax.rem(q + d, Q), col)

    mate = (row, k * 2 + 1 - c)

    def remote(src, dst, send, recv, device):
        return pltpu.make_async_remote_copy(
            src_ref=src, dst_ref=dst, send_sem=send, recv_sem=recv,
            device_id=device, device_id_type=MESH,
        )

    barrier = pltpu.get_barrier_semaphore()
    peers = [at_head(d) for d in range(1, HEADS)] + [at_k(d) for d in range(1, K)]
    peers += [at_q(d) for d in range(1, Q)] + [mate]
    for peer in peers:
        pl.semaphore_signal(barrier, inc=1, device_id=peer, device_id_type=MESH)

    def head_lanes(h):
        return pl.ds(pl.multiple_of(h * HEAD, HEAD), HEAD)

    own_lanes = head_lanes(p)
    own_copies = [
        pltpu.make_async_copy(x.at[:, own_lanes], y, own.at[i])
        for i, (x, y) in enumerate([
            (rep_b, in_b.at[s, p, 0]), (val_b, in_b.at[s, p, 1]),
            (rep_a, in_a.at[p, k, 0]), (val_a, in_a.at[p, k, 1]),
        ])
    ]
    for copy in own_copies:
        copy.start()
    peak_a[...] = jnp.full_like(peak_a, -jnp.inf)
    pl.semaphore_wait(barrier, len(peers))

    def cut_b_copy(d, i):
        return remote(
            (rep_b, val_b)[i].at[:, head_lanes(head_at(d))], in_b.at[s, p, i],
            cut_b_send.at[d, i], b_recv.at[s, p, i], at_head(d),
        )

    def cut_a_copy(d, i):
        return remote(
            (rep_a, val_a)[i].at[:, head_lanes(head_at(d))], in_a.at[p, k, i],
            cut_a_send.at[d, i], a_recv.at[k, p, i], at_head(d),
        )

    def a_copy(d, e, i):
        piece = in_a.at[head_at(e), k, i]
        return remote(piece, piece, a_send.at[d, e, i], a_all.at[k, i], at_k(d))

    def b_copy(d, e, i):
        piece = in_b.at[s, head_at(e), i]
        return remote(piece, piece, b_send.at[d, e, i], b_all.at[s, i], at_q(d))

    def mate_copy(d, i):
        r = lax.rem(q + d, Q) * 2 + c
        block = in_b.at[r, :, i]
        return remote(block, block, mate_send.at[d, i], b_all.at[r, i], mate)

    def pass_b(e, i, own=False):
        if not own:
            piece = in_b.at[s, head_at(e), i]
            remote(
                piece, piece, cut_b_send.at[e, i], b_recv.at[s, head_at(e), i], at_head(e)
            ).wait_recv()
        for d in range(1, Q):
            b_copy(d, e, i).start()

    def wait_b(r, i, device):
        block = in_b.at[r, :, i]
        remote(block, block, mate_send.at[0, i], b_all.at[r, i], device).wait_recv()

    def pass_b_to_mate(i):
        for d in range(1, Q):
            wait_b(lax.rem(q + d, Q) * 2 + c, i, at_q(d))
            mate_copy(d, i).start()

    def pass_a(e, i, own=False):
        if not own:
            piece = in_a.at[head_at(e), k, i]
            remote(
                piece, piece, cut_a_send.at[e, i], a_recv.at[k, head_at(e), i], at_head(e)
            ).wait_recv()
        for d in range(1, K):
            a_copy(d, e, i).start()

    def end_a(i):
        for d in range(1, K):
            block = in_a.at[:, lax.rem(k + d, K), i]
            remote(
                block, block, a_send.at[d, 0, i], a_all.at[lax.rem(k + d, K), i], at_k(d)
            ).wait_recv()

    pl.loop(1, HEADS)(lambda d: cut_a_copy(d, 0).start())
    pl.loop(1, HEADS)(lambda d: cut_b_copy(d, 0).start())
    for copy in own_copies:
        copy.wait()
    pass_a(0, 0, own=True)
    pass_b(0, 0, own=True)
    pl.loop(1, HEADS)(lambda e: pass_a(e, 0))
    pl.loop(1, HEADS)(lambda d: cut_a_copy(d, 1).start())
    pl.loop(1, HEADS)(lambda e: pass_b(e, 0))
    pl.loop(1, HEADS)(lambda d: cut_b_copy(d, 1).start())
    mate_copy(0, 0).start()
    pass_a(0, 1, own=True)
    pass_b(0, 1, own=True)
    end_a(0)

    width = HEADS * n_b
    span = K * n_a
    def rows_at(e):
        return pl.ds(pl.multiple_of(head_at(e) * span, span), span)

    def lane_groups(x):
        return [x[:, j:j + HEAD] for j in range(0, width, HEAD)]

    def score_block(r):
        keys_t = in_b[r, :, 0].reshape(width, HEAD).T
        tops = jnp.full((8, width), -jnp.inf, jnp.float32)
        for h in range(HEADS):
            queries = in_a[h, :, 0].reshape(span, HEAD)
            logits = jnp.dot(queries, keys_t, preferred_element_type=jnp.float32) * to_log2
            scores[r, h * span:(h + 1) * span, :] = logits
            tops = jnp.maximum(tops, jnp.max(logits.reshape(span // 8, 8, width), axis=0))
            peak_a[h] = functools.reduce(jnp.maximum, lane_groups(logits), peak_a[h])
        peak_b[r] = tops

    @pl.loop(0, 2 * Q)
    def _(t):
        @pl.when(t == 1)
        def _():
            pass_b_to_mate(0)

        near = t < Q
        r = lax.rem(q + lax.rem(t, Q), Q) * 2 + jnp.where(near, c, 1 - c)

        @pl.when(t >= Q)
        def _():
            wait_b(r, 0, mate)

        score_block(r)

        @pl.when((t > 0) & (t < HEADS))
        def _():
            pass_a(t, 1)

    for e in range(2 * Q, HEADS):
        pass_a(e, 1)

    def row_block(e):
        pp = head_at(e)
        peak = jnp.max(peak_a[pp], axis=1, keepdims=True)
        totals = jnp.zeros((span, HEAD), jnp.float32)
        num = jnp.zeros((span, HEAD), jnp.float32)
        for r in range(2 * Q):
            values = in_b[r, :, 1].reshape(width, HEAD)
            weights = jnp.exp2(scores[r, rows_at(e), :] - peak)
            totals = functools.reduce(jnp.add, lane_groups(weights), totals)
            num += jnp.dot(
                weights.astype(jnp.bfloat16), values, preferred_element_type=jnp.float32
            )
        total = jnp.sum(totals, axis=1, keepdims=True)
        lane = lax.broadcasted_iota(jnp.int32, (span, HEAD), 1)
        stats = jnp.where(lane == 0, peak, total)
        for kk in range(K):
            mine = slice(kk * n_a, (kk + 1) * n_a)
            num_t = num[mine].T
            stats_t = stats[mine].T[0:STATS]
            part_a[kk, pp, 0:HEAD] = num_t
            part_a[kk, pp, HEAD:HEAD + STATS] = stats_t
            codes, extra = packed_part(num_t, stats_t[1:2], stats_t[0:1])
            code_a[kk, pp, 0:HEAD] = codes
            code_a[kk, pp, HEAD:HEAD + EXTRA] = extra

    def part_a_copy(d, e):
        there = lax.rem(k + d, K)
        h = head_at(e)
        return remote(
            code_a.at[there, h], got_a.at[k, h], part_a_send.at[d, e], got_a_recv.at[k, h], at_k(d)
        )

    end_a(1)
    values_t[...] = in_a[:, :, 1].reshape(HEADS * span, HEAD).T

    def col_block(r):
        peak = jnp.max(peak_b[r], axis=0, keepdims=True)
        weights = jnp.exp2(scores[r] - peak)
        total = jnp.sum(weights, axis=0, keepdims=True)
        num = jnp.dot(values_t[...], weights.astype(jnp.bfloat16), preferred_element_type=jnp.float32)
        sub = lax.broadcasted_iota(jnp.int32, (STATS, width), 0)
        stats = jnp.where(sub == 0, peak, total)
        for h in range(HEADS):
            part_b[r, h, 0:HEAD] = num[:, h * n_b:(h + 1) * n_b]
            part_b[r, h, HEAD:HEAD + STATS] = stats[:, h * n_b:(h + 1) * n_b]

    def mate_b_copy(d):
        qq = lax.rem(q + d, Q)
        return remote(
            part_b.at[qq * 2 + 1 - c], mate_b.at[qq], mate_b_send.at[d], mate_b_recv.at[qq], mate
        )

    def part_b_copy(d, e):
        h = head_at(e)
        return remote(
            code_b.at[lax.rem(q + d, Q), h], got_b.at[q, h], part_b_send.at[d, e], got_b_recv.at[q, h], at_q(d)
        )

    def part_of(ref):
        return ref[0:HEAD], ref[HEAD + 1:HEAD + 2], ref[HEAD:HEAD + 1]

    def sent_part_of(ref):
        return unpacked_part(ref[0:HEAD], ref[HEAD:HEAD + EXTRA])

    def done_copy(e, done, back, send, recv):
        return remote(done.at[head_at(e)], back.at[p], send.at[e], recv.at[p], at_head(e))

    def wait_done(e, done, back, send, recv):
        h = head_at(e)
        remote(done.at[h], back.at[h], send.at[e], recv.at[h], at_head(e)).wait_recv()

    def finish(e, parts, done, back, send, recv):
        num, total, _ = merged(parts)
        result = (num / total).T
        n = result.shape[0]
        scale = scale_of(result)
        codes = code_of(result, scale.astype(jnp.float32))
        extra = jnp.broadcast_to(scale, (EXTRA, HEAD))

        @pl.when(e > 0)
        def _():
            done[head_at(e), 0:n] = codes
            done[head_at(e), n:n + EXTRA] = extra
            done_copy(e, done, back, send, recv).start()

        @pl.when(e == 0)
        def _():
            back[p, 0:n] = codes
            back[p, n:n + EXTRA] = extra

    def finish_a(e):
        h = head_at(e)
        parts = [part_of(part_a.at[k, h])]
        for d in range(1, K):
            kk = lax.rem(k + d, K)
            remote(
                code_a.at[kk, h], got_a.at[kk, h], part_a_send.at[d, e], got_a_recv.at[kk, h],
                at_k(d),
            ).wait_recv()
            parts.append(sent_part_of(got_a.at[kk, h]))
        finish(e, parts, done_a, back_a, done_a_send, done_a_recv)

    def finish_b(e):
        h = head_at(e)
        parts = [part_of(part_b.at[s, h])]
        for d in range(1, Q):
            qq = lax.rem(q + d, Q)
            remote(
                code_b.at[qq, h], got_b.at[qq, h], part_b_send.at[d, e],
                got_b_recv.at[qq, h], at_q(d),
            ).wait_recv()
            parts.append(sent_part_of(got_b.at[qq, h]))
        finish(e, parts, done_b, back_b, done_b_send, done_b_recv)

    def merge_mate(d):
        qq = lax.rem(q + d, Q)
        mate_b_copy(d).wait_recv()

        @pl.loop(0, HEADS)
        def _(e):
            h = head_at(e)
            both = merged([part_of(part_b.at[qq * 2 + c, h]), part_of(mate_b.at[qq, h])])

            @pl.when(d > 0)
            def _():
                codes, extra = packed_part(*both)
                code_b[qq, h, 0:HEAD] = codes
                code_b[qq, h, HEAD:HEAD + EXTRA] = extra
                part_b_copy(d, e).start()

            @pl.when(d == 0)
            def _():
                part_b[qq * 2 + c, h, 0:HEAD] = both[0]
                part_b[qq * 2 + c, h, HEAD:HEAD + 1] = both[2]
                part_b[qq * 2 + c, h, HEAD + 1:HEAD + 2] = both[1]

    @pl.loop(0, 2 * Q)
    def _(t):
        d = lax.rem(t + 1, Q)
        first = t < Q
        col_block(lax.rem(q + d, Q) * 2 + jnp.where(first, 1 - c, c))

        @pl.when(first)
        def _():
            mate_b_copy(d).start()

        @pl.when(t == 0)
        def _():
            pl.loop(1, HEADS)(lambda e: pass_b(e, 1))
            mate_copy(0, 1).start()

        @pl.when(t == Q - 1)
        def _():
            pass_b_to_mate(1)

        @pl.when(t >= Q)
        def _():
            merge_mate(d)

    for d in range(Q):
        wait_b(lax.rem(q + d, Q) * 2 + 1 - c, 1, mate)

    @pl.loop(0, HEADS + 1)
    def _(n):
        @pl.when(n < HEADS)
        def _():
            e = lax.rem(n + 1, HEADS)
            row_block(e)
            for d in range(1, K):
                part_a_copy(d, e).start()

        @pl.when(n > 0)
        def _():
            finish_b(lax.rem(n, HEADS))
            finish_a(lax.rem(n, HEADS))

    @pl.loop(1, HEADS)
    def _(e):
        for i in range(2):
            cut_b_copy(e, i).wait_send()
            cut_a_copy(e, i).wait_send()

    @pl.loop(0, HEADS)
    def _(e):
        for d in range(1, K):
            for i in range(2):
                a_copy(d, e, i).wait_send()
            part_a_copy(d, e).wait_send()
        for d in range(1, Q):
            for i in range(2):
                b_copy(d, e, i).wait_send()
            part_b_copy(d, e).wait_send()

    for d in range(Q):
        for i in range(2):
            mate_copy(d, i).wait_send()
        mate_b_copy(d).wait_send()

    @pl.loop(1, HEADS)
    def _(e):
        done_copy(e, done_a, back_a, done_a_send, done_a_recv).wait_send()
        done_copy(e, done_b, back_b, done_b_send, done_b_recv).wait_send()
        wait_done(e, done_b, back_b, done_b_send, done_b_recv)
        wait_done(e, done_a, back_a, done_a_send, done_a_recv)


def decode(back_a, back_b, out_a, out_b):
    for back, out in ((back_a, out_a), (back_b, out_b)):
        n = out.shape[0]
        for h in range(HEADS):
            scale = back[h, n:n + EXTRA].astype(jnp.float32)[0:1]
            out[:, h * HEAD:(h + 1) * HEAD] = value_of(back[h, 0:n], scale)


def on_device(rows, cols, rep_a, val_a, rep_b, val_b):
    Q, K = rows // HEADS, cols // 2
    n_a, n_b = rep_a.shape[0], rep_b.shape[0]
    f32, bf16 = jnp.float32, jnp.bfloat16
    tall = HEAD + STATS
    dma = pltpu.SemaphoreType.DMA
    vmem = pl.BlockSpec(memory_space=pltpu.VMEM)
    hbm = pl.BlockSpec(memory_space=pltpu.HBM)
    tile = K * HEADS * n_a * 2 * Q * HEADS * n_b
    back_a, back_b = pl.pallas_call(
        functools.partial(kernel, rows, cols),
        out_shape=(
            jax.ShapeDtypeStruct((HEADS, n_a + EXTRA, HEAD), bf16),
            jax.ShapeDtypeStruct((HEADS, n_b + EXTRA, HEAD), bf16),
        ),
        in_specs=[hbm] * 4,
        out_specs=(vmem, vmem),
        scratch_shapes=[
            pltpu.VMEM((HEADS, K, 2, n_a, HEAD), bf16),
            pltpu.VMEM((2 * Q, HEADS, 2, n_b, HEAD), bf16),
            pltpu.VMEM((HEAD, HEADS * K * n_a), bf16),
            pltpu.VMEM((2 * Q, K * HEADS * n_a, HEADS * n_b), f32),
            pltpu.VMEM((HEADS, K * n_a, HEAD), f32),
            pltpu.VMEM((2 * Q, 8, HEADS * n_b), f32),
            pltpu.VMEM((K, HEADS, tall, n_a), f32),
            pltpu.VMEM((K, HEADS, HEAD + EXTRA, n_a), bf16),
            pltpu.VMEM((K, HEADS, HEAD + EXTRA, n_a), bf16),
            pltpu.VMEM((2 * Q, HEADS, tall, n_b), f32),
            pltpu.VMEM((Q, HEADS, tall, n_b), f32),
            pltpu.VMEM((Q, HEADS, HEAD + EXTRA, n_b), bf16),
            pltpu.VMEM((Q, HEADS, HEAD + EXTRA, n_b), bf16),
            pltpu.VMEM((HEADS, n_a + EXTRA, HEAD), bf16),
            pltpu.VMEM((HEADS, n_b + EXTRA, HEAD), bf16),
            dma((4,)), dma((HEADS, 2)), dma((HEADS, 2)),
            dma((K, HEADS, 2)), dma((2 * Q, HEADS, 2)),
            dma((K, 2)), dma((2 * Q, 2)),
            dma((K, HEADS, 2)), dma((Q, HEADS, 2)), dma((Q, 2)),
            dma((K, HEADS)), dma((K, HEADS)),
            dma((Q,)), dma((Q,)),
            dma((Q, HEADS)), dma((Q, HEADS)),
            dma((HEADS,)), dma((HEADS,)), dma((HEADS,)), dma((HEADS,)),
        ],
        compiler_params=pltpu.CompilerParams(
            collective_id=0, has_side_effects=True, vmem_limit_bytes=GRANT
        ),
        cost_estimate=pl.CostEstimate(
            flops=6 * tile * HEAD, bytes_accessed=6 * 1024 * (n_a + n_b), transcendentals=2 * tile
        ),
    )(rep_a, val_a, rep_b, val_b)
    return pl.pallas_call(
        decode,
        out_shape=(
            jax.ShapeDtypeStruct(rep_a.shape, f32),
            jax.ShapeDtypeStruct(rep_b.shape, f32),
        ),
        in_specs=[vmem] * 2,
        out_specs=(vmem, vmem),
        compiler_params=pltpu.CompilerParams(vmem_limit_bytes=GRANT),
    )(back_a, back_b)


def solution(mesh):
    rows, cols = mesh.shape["row"], mesh.shape["col"]
    placed = P(("row", "col"), None)
    return jax.shard_map(
        functools.partial(on_device, rows, cols),
        mesh=mesh,
        in_specs=(placed,) * 4,
        out_specs=(placed, placed),
        check_vma=False,
    )
```

```python
import functools
import math

import jax
import jax.numpy as jnp
from jax import lax
from jax.experimental import pallas as pl
from jax.experimental.pallas import tpu as pltpu
from jax.sharding import PartitionSpec as P

HEADS = 4
HEAD = 128
STATS = 8
EXTRA = 16
BINADES = 248.0
GRANT = 127 * 512 * 1024
MESH = pl.DeviceIdType.MESH


def code_of(x, scale):
    code = jnp.exp2(jnp.abs(x) * (BINADES / scale) - BINADES / 2)
    return jnp.where(x < 0, -code, code).astype(jnp.bfloat16)


def value_of(code, scale):
    code = code.astype(jnp.float32)
    size = jnp.log(jnp.abs(code)) * (1 / (math.log(2) * BINADES)) + 0.5
    return jnp.where(code < 0, -size, size) * scale


def scale_of(x):
    largest = jnp.max(jnp.abs(x), axis=0, keepdims=True) * 1.01 + 1e-30
    return largest.astype(jnp.bfloat16)


def three_terms(x):
    terms = []
    for _ in range(3):
        term = x.astype(jnp.bfloat16).astype(jnp.float32)
        terms.append(term)
        x = x - term
    return terms


def packed_part(num, total, peak):
    mean = num / total
    scale = scale_of(mean).astype(jnp.float32)
    rows = [scale] + three_terms(peak) + three_terms(total)
    sub = lax.broadcasted_iota(jnp.int32, (EXTRA, num.shape[1]), 0)
    extra = jnp.zeros((EXTRA, num.shape[1]), jnp.float32)
    for i, x in enumerate(rows):
        extra = jnp.where(sub == i, x, extra)
    return code_of(mean, scale), extra.astype(jnp.bfloat16)


def unpacked_part(codes, extra):
    extra = extra.astype(jnp.float32)
    peak = extra[1:2] + extra[2:3] + extra[3:4]
    total = extra[4:5] + extra[5:6] + extra[6:7]
    return value_of(codes, extra[0:1]) * total, total, peak


def merged(parts):
    peak = functools.reduce(jnp.maximum, [x[2] for x in parts])
    scales = [jnp.exp2(x[2] - peak) for x in parts]
    num = sum(x[0] * w for x, w in zip(parts, scales))
    total = sum(x[1] * w for x, w in zip(parts, scales))
    return num, total, peak


def kernel(
    rows, cols,
    rep_a, val_a, rep_b, val_b, back_a, back_b,
    in_a, in_b, values_t, scores, peak_a, peak_b,
    part_a, code_a, got_a, part_b, mate_b, code_b, got_b, done_a, done_b,
    own, cut_a_send, cut_b_send, a_recv, b_recv, a_all, b_all, a_send, b_send, mate_send,
    part_a_send, got_a_recv, mate_b_send, mate_b_recv, part_b_send, got_b_recv,
    done_a_send, done_b_send, done_a_recv, done_b_recv,
):
    Q, K = rows // HEADS, cols // 2
    n_a, n_b = rep_a.shape[0], rep_b.shape[0]
    row, col = lax.axis_index("row"), lax.axis_index("col")
    p, q = lax.div(row, Q), lax.rem(row, Q)
    k, c = lax.div(col, 2), lax.rem(col, 2)
    s = q * 2 + c
    to_log2 = HEAD ** -0.5 * math.log2(math.e)

    def head_at(d):
        return lax.rem(p + d, HEADS)

    def at_head(d):
        return (head_at(d) * Q + q, col)

    def at_k(d):
        return (row, lax.rem(k + d, K) * 2 + c)

    def at_q(d):
        return (p * Q + lax.rem(q + d, Q), col)

    mate = (row, k * 2 + 1 - c)

    def remote(src, dst, send, recv, device):
        return pltpu.make_async_remote_copy(
            src_ref=src, dst_ref=dst, send_sem=send, recv_sem=recv,
            device_id=device, device_id_type=MESH,
        )

    barrier = pltpu.get_barrier_semaphore()
    peers = [at_head(d) for d in range(1, HEADS)] + [at_k(d) for d in range(1, K)]
    peers += [at_q(d) for d in range(1, Q)] + [mate]
    for peer in peers:
        pl.semaphore_signal(barrier, inc=1, device_id=peer, device_id_type=MESH)

    def head_lanes(h):
        return pl.ds(pl.multiple_of(h * HEAD, HEAD), HEAD)

    own_lanes = head_lanes(p)
    own_copies = [
        pltpu.make_async_copy(x.at[:, own_lanes], y, own.at[i])
        for i, (x, y) in enumerate([
            (rep_b, in_b.at[s, p, 0]), (val_b, in_b.at[s, p, 1]),
            (rep_a, in_a.at[p, k, 0]), (val_a, in_a.at[p, k, 1]),
        ])
    ]
    for copy in own_copies:
        copy.start()
    peak_a[...] = jnp.full_like(peak_a, -jnp.inf)
    pl.semaphore_wait(barrier, len(peers))

    def cut_b_copy(d, i):
        return remote(
            (rep_b, val_b)[i].at[:, head_lanes(head_at(d))], in_b.at[s, p, i],
            cut_b_send.at[d, i], b_recv.at[s, p, i], at_head(d),
        )

    def cut_a_copy(d, i):
        return remote(
            (rep_a, val_a)[i].at[:, head_lanes(head_at(d))], in_a.at[p, k, i],
            cut_a_send.at[d, i], a_recv.at[k, p, i], at_head(d),
        )

    def a_copy(d, e, i):
        piece = in_a.at[head_at(e), k, i]
        return remote(piece, piece, a_send.at[d, e, i], a_all.at[k, i], at_k(d))

    def b_copy(d, e, i):
        piece = in_b.at[s, head_at(e), i]
        return remote(piece, piece, b_send.at[d, e, i], b_all.at[s, i], at_q(d))

    def mate_copy(d, i):
        r = lax.rem(q + d, Q) * 2 + c
        block = in_b.at[r, :, i]
        return remote(block, block, mate_send.at[d, i], b_all.at[r, i], mate)

    def pass_b(e, i, own=False):
        if not own:
            piece = in_b.at[s, head_at(e), i]
            remote(
                piece, piece, cut_b_send.at[e, i], b_recv.at[s, head_at(e), i], at_head(e)
            ).wait_recv()
        for d in range(1, Q):
            b_copy(d, e, i).start()

    def wait_b(r, i, device):
        block = in_b.at[r, :, i]
        remote(block, block, mate_send.at[0, i], b_all.at[r, i], device).wait_recv()

    def pass_b_to_mate(i):
        for d in range(1, Q):
            wait_b(lax.rem(q + d, Q) * 2 + c, i, at_q(d))
            mate_copy(d, i).start()

    def pass_a(e, i, own=False):
        if not own:
            piece = in_a.at[head_at(e), k, i]
            remote(
                piece, piece, cut_a_send.at[e, i], a_recv.at[k, head_at(e), i], at_head(e)
            ).wait_recv()
        for d in range(1, K):
            a_copy(d, e, i).start()

    def end_a(i):
        for d in range(1, K):
            block = in_a.at[:, lax.rem(k + d, K), i]
            remote(
                block, block, a_send.at[d, 0, i], a_all.at[lax.rem(k + d, K), i], at_k(d)
            ).wait_recv()

    pl.loop(1, HEADS)(lambda d: cut_a_copy(d, 0).start())
    pl.loop(1, HEADS)(lambda d: cut_b_copy(d, 0).start())
    for copy in own_copies:
        copy.wait()
    pass_a(0, 0, own=True)
    pass_b(0, 0, own=True)
    pl.loop(1, HEADS)(lambda e: pass_a(e, 0))
    pl.loop(1, HEADS)(lambda d: cut_a_copy(d, 1).start())
    pl.loop(1, HEADS)(lambda e: pass_b(e, 0))
    pl.loop(1, HEADS)(lambda d: cut_b_copy(d, 1).start())
    mate_copy(0, 0).start()
    pass_a(0, 1, own=True)
    pass_b(0, 1, own=True)
    end_a(0)

    width = HEADS * n_b
    span = K * n_a
    def rows_at(e):
        return pl.ds(pl.multiple_of(head_at(e) * span, span), span)

    def lane_groups(x):
        return [x[:, j:j + HEAD] for j in range(0, width, HEAD)]

    def score_block(r):
        keys_t = in_b[r, :, 0].reshape(width, HEAD).T
        tops = jnp.full((8, width), -jnp.inf, jnp.float32)
        for h in range(HEADS):
            queries = in_a[h, :, 0].reshape(span, HEAD)
            logits = jnp.dot(queries, keys_t, preferred_element_type=jnp.float32) * to_log2
            scores[r, h * span:(h + 1) * span, :] = logits
            tops = jnp.maximum(tops, jnp.max(logits.reshape(span // 8, 8, width), axis=0))
            peak_a[h] = functools.reduce(jnp.maximum, lane_groups(logits), peak_a[h])
        peak_b[r] = tops

    @pl.loop(0, 2 * Q)
    def _(t):
        @pl.when(t == 1)
        def _():
            pass_b_to_mate(0)

        near = t < Q
        r = lax.rem(q + lax.rem(t, Q), Q) * 2 + jnp.where(near, c, 1 - c)

        @pl.when(t >= Q)
        def _():
            wait_b(r, 0, mate)

        score_block(r)

        @pl.when(t == 2 * Q - 2)
        def _():
            pl.loop(1, HEADS)(lambda e: pass_a(e, 1))

    def row_block(e):
        pp = head_at(e)
        peak = jnp.max(peak_a[pp], axis=1, keepdims=True)
        totals = jnp.zeros((span, HEAD), jnp.float32)
        num = jnp.zeros((span, HEAD), jnp.float32)
        for r in range(2 * Q):
            values = in_b[r, :, 1].reshape(width, HEAD)
            weights = jnp.exp2(scores[r, rows_at(e), :] - peak)
            totals = functools.reduce(jnp.add, lane_groups(weights), totals)
            num += jnp.dot(
                weights.astype(jnp.bfloat16), values, preferred_element_type=jnp.float32
            )
        total = jnp.sum(totals, axis=1, keepdims=True)
        lane = lax.broadcasted_iota(jnp.int32, (span, HEAD), 1)
        stats = jnp.where(lane == 0, peak, total)
        for kk in range(K):
            mine = slice(kk * n_a, (kk + 1) * n_a)
            num_t = num[mine].T
            stats_t = stats[mine].T[0:STATS]
            part_a[kk, pp, 0:HEAD] = num_t
            part_a[kk, pp, HEAD:HEAD + STATS] = stats_t
            codes, extra = packed_part(num_t, stats_t[1:2], stats_t[0:1])
            code_a[kk, pp, 0:HEAD] = codes
            code_a[kk, pp, HEAD:HEAD + EXTRA] = extra

    def part_a_copy(d, e):
        there = lax.rem(k + d, K)
        h = head_at(e)
        return remote(
            code_a.at[there, h], got_a.at[k, h], part_a_send.at[d, e], got_a_recv.at[k, h], at_k(d)
        )

    end_a(1)
    values_t[...] = in_a[:, :, 1].reshape(HEADS * span, HEAD).T

    def col_block(r):
        peak = jnp.max(peak_b[r], axis=0, keepdims=True)
        weights = jnp.exp2(scores[r] - peak)
        total = jnp.sum(weights, axis=0, keepdims=True)
        num = jnp.dot(values_t[...], weights.astype(jnp.bfloat16), preferred_element_type=jnp.float32)
        sub = lax.broadcasted_iota(jnp.int32, (STATS, width), 0)
        stats = jnp.where(sub == 0, peak, total)
        for h in range(HEADS):
            part_b[r, h, 0:HEAD] = num[:, h * n_b:(h + 1) * n_b]
            part_b[r, h, HEAD:HEAD + STATS] = stats[:, h * n_b:(h + 1) * n_b]

    def mate_b_copy(d):
        qq = lax.rem(q + d, Q)
        return remote(
            part_b.at[qq * 2 + 1 - c], mate_b.at[qq], mate_b_send.at[d], mate_b_recv.at[qq], mate
        )

    def part_b_copy(d, e):
        h = head_at(e)
        return remote(
            code_b.at[lax.rem(q + d, Q), h], got_b.at[q, h], part_b_send.at[d, e], got_b_recv.at[q, h], at_q(d)
        )

    def part_of(ref):
        return ref[0:HEAD], ref[HEAD + 1:HEAD + 2], ref[HEAD:HEAD + 1]

    def sent_part_of(ref):
        return unpacked_part(ref[0:HEAD], ref[HEAD:HEAD + EXTRA])

    def done_copy(e, done, back, send, recv):
        return remote(done.at[head_at(e)], back.at[p], send.at[e], recv.at[p], at_head(e))

    def wait_done(e, done, back, send, recv):
        h = head_at(e)
        remote(done.at[h], back.at[h], send.at[e], recv.at[h], at_head(e)).wait_recv()

    def finish(e, parts, done, back, send, recv):
        num, total, _ = merged(parts)
        result = (num / total).T
        n = result.shape[0]
        scale = scale_of(result)
        codes = code_of(result, scale.astype(jnp.float32))
        extra = jnp.broadcast_to(scale, (EXTRA, HEAD))

        @pl.when(e > 0)
        def _():
            done[head_at(e), 0:n] = codes
            done[head_at(e), n:n + EXTRA] = extra
            done_copy(e, done, back, send, recv).start()

        @pl.when(e == 0)
        def _():
            back[p, 0:n] = codes
            back[p, n:n + EXTRA] = extra

    def finish_a(e):
        h = head_at(e)
        parts = [part_of(part_a.at[k, h])]
        for d in range(1, K):
            kk = lax.rem(k + d, K)
            remote(
                code_a.at[kk, h], got_a.at[kk, h], part_a_send.at[d, e], got_a_recv.at[kk, h],
                at_k(d),
            ).wait_recv()
            parts.append(sent_part_of(got_a.at[kk, h]))
        finish(e, parts, done_a, back_a, done_a_send, done_a_recv)

    def finish_b(e):
        h = head_at(e)
        parts = [part_of(part_b.at[s, h])]
        for d in range(1, Q):
            qq = lax.rem(q + d, Q)
            remote(
                code_b.at[qq, h], got_b.at[qq, h], part_b_send.at[d, e],
                got_b_recv.at[qq, h], at_q(d),
            ).wait_recv()
            parts.append(sent_part_of(got_b.at[qq, h]))
        finish(e, parts, done_b, back_b, done_b_send, done_b_recv)

    def merge_mate(d):
        qq = lax.rem(q + d, Q)
        mate_b_copy(d).wait_recv()

        @pl.loop(0, HEADS)
        def _(e):
            h = head_at(e)
            both = merged([part_of(part_b.at[qq * 2 + c, h]), part_of(mate_b.at[qq, h])])

            @pl.when(d > 0)
            def _():
                codes, extra = packed_part(*both)
                code_b[qq, h, 0:HEAD] = codes
                code_b[qq, h, HEAD:HEAD + EXTRA] = extra
                part_b_copy(d, e).start()

            @pl.when(d == 0)
            def _():
                part_b[qq * 2 + c, h, 0:HEAD] = both[0]
                part_b[qq * 2 + c, h, HEAD:HEAD + 1] = both[2]
                part_b[qq * 2 + c, h, HEAD + 1:HEAD + 2] = both[1]

    @pl.loop(0, 2 * Q)
    def _(t):
        d = lax.rem(t + 1, Q)
        first = t < Q
        col_block(lax.rem(q + d, Q) * 2 + jnp.where(first, 1 - c, c))

        @pl.when(first)
        def _():
            mate_b_copy(d).start()

        @pl.when(t == 0)
        def _():
            pl.loop(1, HEADS)(lambda e: pass_b(e, 1))
            mate_copy(0, 1).start()

        @pl.when(t == Q)
        def _():
            pass_b_to_mate(1)

        @pl.when(t >= Q)
        def _():
            merge_mate(d)

    for d in range(Q):
        wait_b(lax.rem(q + d, Q) * 2 + 1 - c, 1, mate)

    @pl.loop(0, HEADS + 1)
    def _(n):
        @pl.when(n < HEADS)
        def _():
            e = lax.rem(n + 1, HEADS)
            row_block(e)
            for d in range(1, K):
                part_a_copy(d, e).start()

        @pl.when(n > 0)
        def _():
            finish_b(lax.rem(n, HEADS))
            finish_a(lax.rem(n, HEADS))

    @pl.loop(1, HEADS)
    def _(e):
        for i in range(2):
            cut_b_copy(e, i).wait_send()
            cut_a_copy(e, i).wait_send()

    @pl.loop(0, HEADS)
    def _(e):
        for d in range(1, K):
            for i in range(2):
                a_copy(d, e, i).wait_send()
            part_a_copy(d, e).wait_send()
        for d in range(1, Q):
            for i in range(2):
                b_copy(d, e, i).wait_send()
            part_b_copy(d, e).wait_send()

    for d in range(Q):
        for i in range(2):
            mate_copy(d, i).wait_send()
        mate_b_copy(d).wait_send()

    @pl.loop(1, HEADS)
    def _(e):
        done_copy(e, done_a, back_a, done_a_send, done_a_recv).wait_send()
        done_copy(e, done_b, back_b, done_b_send, done_b_recv).wait_send()
        wait_done(e, done_b, back_b, done_b_send, done_b_recv)
        wait_done(e, done_a, back_a, done_a_send, done_a_recv)


def decode(back_a, back_b, out_a, out_b):
    for back, out in ((back_a, out_a), (back_b, out_b)):
        n = out.shape[0]
        for h in range(HEADS):
            scale = back[h, n:n + EXTRA].astype(jnp.float32)[0:1]
            out[:, h * HEAD:(h + 1) * HEAD] = value_of(back[h, 0:n], scale)


def on_device(rows, cols, rep_a, val_a, rep_b, val_b):
    Q, K = rows // HEADS, cols // 2
    n_a, n_b = rep_a.shape[0], rep_b.shape[0]
    f32, bf16 = jnp.float32, jnp.bfloat16
    tall = HEAD + STATS
    dma = pltpu.SemaphoreType.DMA
    vmem = pl.BlockSpec(memory_space=pltpu.VMEM)
    hbm = pl.BlockSpec(memory_space=pltpu.HBM)
    tile = K * HEADS * n_a * 2 * Q * HEADS * n_b
    back_a, back_b = pl.pallas_call(
        functools.partial(kernel, rows, cols),
        out_shape=(
            jax.ShapeDtypeStruct((HEADS, n_a + EXTRA, HEAD), bf16),
            jax.ShapeDtypeStruct((HEADS, n_b + EXTRA, HEAD), bf16),
        ),
        in_specs=[hbm] * 4,
        out_specs=(vmem, vmem),
        scratch_shapes=[
            pltpu.VMEM((HEADS, K, 2, n_a, HEAD), bf16),
            pltpu.VMEM((2 * Q, HEADS, 2, n_b, HEAD), bf16),
            pltpu.VMEM((HEAD, HEADS * K * n_a), bf16),
            pltpu.VMEM((2 * Q, K * HEADS * n_a, HEADS * n_b), f32),
            pltpu.VMEM((HEADS, K * n_a, HEAD), f32),
            pltpu.VMEM((2 * Q, 8, HEADS * n_b), f32),
            pltpu.VMEM((K, HEADS, tall, n_a), f32),
            pltpu.VMEM((K, HEADS, HEAD + EXTRA, n_a), bf16),
            pltpu.VMEM((K, HEADS, HEAD + EXTRA, n_a), bf16),
            pltpu.VMEM((2 * Q, HEADS, tall, n_b), f32),
            pltpu.VMEM((Q, HEADS, tall, n_b), f32),
            pltpu.VMEM((Q, HEADS, HEAD + EXTRA, n_b), bf16),
            pltpu.VMEM((Q, HEADS, HEAD + EXTRA, n_b), bf16),
            pltpu.VMEM((HEADS, n_a + EXTRA, HEAD), bf16),
            pltpu.VMEM((HEADS, n_b + EXTRA, HEAD), bf16),
            dma((4,)), dma((HEADS, 2)), dma((HEADS, 2)),
            dma((K, HEADS, 2)), dma((2 * Q, HEADS, 2)),
            dma((K, 2)), dma((2 * Q, 2)),
            dma((K, HEADS, 2)), dma((Q, HEADS, 2)), dma((Q, 2)),
            dma((K, HEADS)), dma((K, HEADS)),
            dma((Q,)), dma((Q,)),
            dma((Q, HEADS)), dma((Q, HEADS)),
            dma((HEADS,)), dma((HEADS,)), dma((HEADS,)), dma((HEADS,)),
        ],
        compiler_params=pltpu.CompilerParams(
            collective_id=0, has_side_effects=True, vmem_limit_bytes=GRANT
        ),
        cost_estimate=pl.CostEstimate(
            flops=6 * tile * HEAD, bytes_accessed=6 * 1024 * (n_a + n_b), transcendentals=2 * tile
        ),
    )(rep_a, val_a, rep_b, val_b)
    return pl.pallas_call(
        decode,
        out_shape=(
            jax.ShapeDtypeStruct(rep_a.shape, f32),
            jax.ShapeDtypeStruct(rep_b.shape, f32),
        ),
        in_specs=[vmem] * 2,
        out_specs=(vmem, vmem),
        compiler_params=pltpu.CompilerParams(vmem_limit_bytes=GRANT),
    )(back_a, back_b)


def solution(mesh):
    rows, cols = mesh.shape["row"], mesh.shape["col"]
    placed = P(("row", "col"), None)
    return jax.shard_map(
        functools.partial(on_device, rows, cols),
        mesh=mesh,
        in_specs=(placed,) * 4,
        out_specs=(placed, placed),
        check_vma=False,
    )
```

```python
import functools
import math

import jax
import jax.numpy as jnp
from jax import lax
from jax.experimental import pallas as pl
from jax.experimental.pallas import tpu as pltpu
from jax.sharding import PartitionSpec as P

HEADS = 4
HEAD = 128
STATS = 8
EXTRA = 16
BINADES = 248.0
GRANT = 127 * 512 * 1024
MESH = pl.DeviceIdType.MESH


def code_of(x, scale):
    code = jnp.exp2(jnp.abs(x) * (BINADES / scale) - BINADES / 2)
    return jnp.where(x < 0, -code, code).astype(jnp.bfloat16)


def value_of(code, scale):
    code = code.astype(jnp.float32)
    size = jnp.log(jnp.abs(code)) * (1 / (math.log(2) * BINADES)) + 0.5
    return jnp.where(code < 0, -size, size) * scale


def scale_of(x):
    largest = jnp.max(jnp.abs(x), axis=0, keepdims=True) * 1.01 + 1e-30
    return largest.astype(jnp.bfloat16)


def three_terms(x):
    terms = []
    for _ in range(3):
        term = x.astype(jnp.bfloat16).astype(jnp.float32)
        terms.append(term)
        x = x - term
    return terms


def packed_part(num, total, peak):
    mean = num / total
    scale = scale_of(mean).astype(jnp.float32)
    rows = [scale] + three_terms(peak) + three_terms(total)
    sub = lax.broadcasted_iota(jnp.int32, (EXTRA, num.shape[1]), 0)
    extra = jnp.zeros((EXTRA, num.shape[1]), jnp.float32)
    for i, x in enumerate(rows):
        extra = jnp.where(sub == i, x, extra)
    return code_of(mean, scale), extra.astype(jnp.bfloat16)


def unpacked_part(codes, extra):
    extra = extra.astype(jnp.float32)
    peak = extra[1:2] + extra[2:3] + extra[3:4]
    total = extra[4:5] + extra[5:6] + extra[6:7]
    return value_of(codes, extra[0:1]) * total, total, peak


def merged(parts):
    peak = functools.reduce(jnp.maximum, [x[2] for x in parts])
    scales = [jnp.exp2(x[2] - peak) for x in parts]
    num = sum(x[0] * w for x, w in zip(parts, scales))
    total = sum(x[1] * w for x, w in zip(parts, scales))
    return num, total, peak


def kernel(
    rows, cols,
    rep_a, val_a, rep_b, val_b, back_a, back_b,
    in_a, in_b, values_t, scores, peak_a, peak_b,
    part_a, code_a, got_a, part_b, mate_b, code_b, got_b, done_a, done_b,
    own, cut_a_send, cut_b_send, a_recv, b_recv, a_all, b_all, a_send, b_send, mate_send,
    part_a_send, got_a_recv, mate_b_send, mate_b_recv, part_b_send, got_b_recv,
    done_a_send, done_b_send, done_a_recv, done_b_recv,
):
    Q, K = rows // HEADS, cols // 2
    n_a, n_b = rep_a.shape[0], rep_b.shape[0]
    row, col = lax.axis_index("row"), lax.axis_index("col")
    p, q = lax.div(row, Q), lax.rem(row, Q)
    k, c = lax.div(col, 2), lax.rem(col, 2)
    s = q * 2 + c
    to_log2 = HEAD ** -0.5 * math.log2(math.e)

    def head_at(d):
        return lax.rem(p + d, HEADS)

    def at_head(d):
        return (head_at(d) * Q + q, col)

    def at_k(d):
        return (row, lax.rem(k + d, K) * 2 + c)

    def at_q(d):
        return (p * Q + lax.rem(q + d, Q), col)

    mate = (row, k * 2 + 1 - c)

    def remote(src, dst, send, recv, device):
        return pltpu.make_async_remote_copy(
            src_ref=src, dst_ref=dst, send_sem=send, recv_sem=recv,
            device_id=device, device_id_type=MESH,
        )

    barrier = pltpu.get_barrier_semaphore()
    peers = [at_head(d) for d in range(1, HEADS)] + [at_k(d) for d in range(1, K)]
    peers += [at_q(d) for d in range(1, Q)] + [mate]
    for peer in peers:
        pl.semaphore_signal(barrier, inc=1, device_id=peer, device_id_type=MESH)

    def head_lanes(h):
        return pl.ds(pl.multiple_of(h * HEAD, HEAD), HEAD)

    own_lanes = head_lanes(p)
    own_copies = [
        pltpu.make_async_copy(x.at[:, own_lanes], y, own.at[i])
        for i, (x, y) in enumerate([
            (rep_b, in_b.at[s, p, 0]), (val_b, in_b.at[s, p, 1]),
            (rep_a, in_a.at[p, k, 0]), (val_a, in_a.at[p, k, 1]),
        ])
    ]
    for copy in own_copies:
        copy.start()
    peak_a[...] = jnp.full_like(peak_a, -jnp.inf)
    pl.semaphore_wait(barrier, len(peers))

    def cut_b_copy(d, i):
        return remote(
            (rep_b, val_b)[i].at[:, head_lanes(head_at(d))], in_b.at[s, p, i],
            cut_b_send.at[d, i], b_recv.at[s, p, i], at_head(d),
        )

    def cut_a_copy(d, i):
        return remote(
            (rep_a, val_a)[i].at[:, head_lanes(head_at(d))], in_a.at[p, k, i],
            cut_a_send.at[d, i], a_recv.at[k, p, i], at_head(d),
        )

    def a_copy(d, e, i):
        piece = in_a.at[head_at(e), k, i]
        return remote(piece, piece, a_send.at[d, e, i], a_all.at[k, i], at_k(d))

    def b_copy(d, e, i):
        piece = in_b.at[s, head_at(e), i]
        return remote(piece, piece, b_send.at[d, e, i], b_all.at[s, i], at_q(d))

    def mate_copy(d, i):
        r = lax.rem(q + d, Q) * 2 + c
        block = in_b.at[r, :, i]
        return remote(block, block, mate_send.at[d, i], b_all.at[r, i], mate)

    def pass_b(e, i, own=False):
        if not own:
            piece = in_b.at[s, head_at(e), i]
            remote(
                piece, piece, cut_b_send.at[e, i], b_recv.at[s, head_at(e), i], at_head(e)
            ).wait_recv()
        for d in range(1, Q):
            b_copy(d, e, i).start()

    def wait_b(r, i, device):
        block = in_b.at[r, :, i]
        remote(block, block, mate_send.at[0, i], b_all.at[r, i], device).wait_recv()

    def pass_b_to_mate(i):
        for d in range(1, Q):
            wait_b(lax.rem(q + d, Q) * 2 + c, i, at_q(d))
            mate_copy(d, i).start()

    def pass_a(e, i, own=False):
        if not own:
            piece = in_a.at[head_at(e), k, i]
            remote(
                piece, piece, cut_a_send.at[e, i], a_recv.at[k, head_at(e), i], at_head(e)
            ).wait_recv()
        for d in range(1, K):
            a_copy(d, e, i).start()

    def end_a(i):
        for d in range(1, K):
            block = in_a.at[:, lax.rem(k + d, K), i]
            remote(
                block, block, a_send.at[d, 0, i], a_all.at[lax.rem(k + d, K), i], at_k(d)
            ).wait_recv()

    pl.loop(1, HEADS)(lambda d: cut_a_copy(d, 0).start())
    for copy in own_copies:
        copy.wait()
    pass_a(0, 0, own=True)
    pass_b(0, 0, own=True)
    pass_a(1, 0)
    pl.loop(1, HEADS)(lambda d: cut_b_copy(d, 0).start())
    pl.loop(2, HEADS)(lambda e: pass_a(e, 0))
    pass_b(1, 0)
    pl.loop(1, HEADS)(lambda d: cut_a_copy(d, 1).start())
    pl.loop(2, HEADS)(lambda e: pass_b(e, 0))
    pl.loop(1, HEADS)(lambda d: cut_b_copy(d, 1).start())
    mate_copy(0, 0).start()
    pass_a(0, 1, own=True)
    pass_b(0, 1, own=True)
    end_a(0)

    width = HEADS * n_b
    span = K * n_a
    def rows_at(e):
        return pl.ds(pl.multiple_of(head_at(e) * span, span), span)

    def lane_groups(x):
        return [x[:, j:j + HEAD] for j in range(0, width, HEAD)]

    def score_block(r):
        keys_t = in_b[r, :, 0].reshape(width, HEAD).T
        tops = jnp.full((8, width), -jnp.inf, jnp.float32)
        for h in range(HEADS):
            queries = in_a[h, :, 0].reshape(span, HEAD)
            logits = jnp.dot(queries, keys_t, preferred_element_type=jnp.float32) * to_log2
            scores[r, h * span:(h + 1) * span, :] = logits
            tops = jnp.maximum(tops, jnp.max(logits.reshape(span // 8, 8, width), axis=0))
            peak_a[h] = functools.reduce(jnp.maximum, lane_groups(logits), peak_a[h])
        peak_b[r] = tops

    @pl.loop(0, 2 * Q)
    def _(t):
        @pl.when(t == 1)
        def _():
            pass_b_to_mate(0)

        near = t < Q
        r = lax.rem(q + lax.rem(t, Q), Q) * 2 + jnp.where(near, c, 1 - c)

        @pl.when(t >= Q)
        def _():
            wait_b(r, 0, mate)

        score_block(r)

        @pl.when(t == 2 * Q - 2)
        def _():
            pl.loop(1, HEADS)(lambda e: pass_a(e, 1))

    def row_block(e):
        pp = head_at(e)
        peak = jnp.max(peak_a[pp], axis=1, keepdims=True)
        totals = jnp.zeros((span, HEAD), jnp.float32)
        num = jnp.zeros((span, HEAD), jnp.float32)
        for r in range(2 * Q):
            values = in_b[r, :, 1].reshape(width, HEAD)
            weights = jnp.exp2(scores[r, rows_at(e), :] - peak)
            totals = functools.reduce(jnp.add, lane_groups(weights), totals)
            num += jnp.dot(
                weights.astype(jnp.bfloat16), values, preferred_element_type=jnp.float32
            )
        total = jnp.sum(totals, axis=1, keepdims=True)
        lane = lax.broadcasted_iota(jnp.int32, (span, HEAD), 1)
        stats = jnp.where(lane == 0, peak, total)
        for kk in range(K):
            mine = slice(kk * n_a, (kk + 1) * n_a)
            num_t = num[mine].T
            stats_t = stats[mine].T[0:STATS]
            part_a[kk, pp, 0:HEAD] = num_t
            part_a[kk, pp, HEAD:HEAD + STATS] = stats_t
            codes, extra = packed_part(num_t, stats_t[1:2], stats_t[0:1])
            code_a[kk, pp, 0:HEAD] = codes
            code_a[kk, pp, HEAD:HEAD + EXTRA] = extra

    def part_a_copy(d, e):
        there = lax.rem(k + d, K)
        h = head_at(e)
        return remote(
            code_a.at[there, h], got_a.at[k, h], part_a_send.at[d, e], got_a_recv.at[k, h], at_k(d)
        )

    end_a(1)
    values_t[...] = in_a[:, :, 1].reshape(HEADS * span, HEAD).T

    def col_block(r):
        peak = jnp.max(peak_b[r], axis=0, keepdims=True)
        weights = jnp.exp2(scores[r] - peak)
        total = jnp.sum(weights, axis=0, keepdims=True)
        num = jnp.dot(values_t[...], weights.astype(jnp.bfloat16), preferred_element_type=jnp.float32)
        sub = lax.broadcasted_iota(jnp.int32, (STATS, width), 0)
        stats = jnp.where(sub == 0, peak, total)
        for h in range(HEADS):
            part_b[r, h, 0:HEAD] = num[:, h * n_b:(h + 1) * n_b]
            part_b[r, h, HEAD:HEAD + STATS] = stats[:, h * n_b:(h + 1) * n_b]

    def mate_b_copy(d):
        qq = lax.rem(q + d, Q)
        return remote(
            part_b.at[qq * 2 + 1 - c], mate_b.at[qq], mate_b_send.at[d], mate_b_recv.at[qq], mate
        )

    def part_b_copy(d, e):
        h = head_at(e)
        return remote(
            code_b.at[lax.rem(q + d, Q), h], got_b.at[q, h], part_b_send.at[d, e], got_b_recv.at[q, h], at_q(d)
        )

    def part_of(ref):
        return ref[0:HEAD], ref[HEAD + 1:HEAD + 2], ref[HEAD:HEAD + 1]

    def sent_part_of(ref):
        return unpacked_part(ref[0:HEAD], ref[HEAD:HEAD + EXTRA])

    def done_copy(e, done, back, send, recv):
        return remote(done.at[head_at(e)], back.at[p], send.at[e], recv.at[p], at_head(e))

    def wait_done(e, done, back, send, recv):
        h = head_at(e)
        remote(done.at[h], back.at[h], send.at[e], recv.at[h], at_head(e)).wait_recv()

    def finish(e, parts, done, back, send, recv):
        num, total, _ = merged(parts)
        result = (num / total).T
        n = result.shape[0]
        scale = scale_of(result)
        codes = code_of(result, scale.astype(jnp.float32))
        extra = jnp.broadcast_to(scale, (EXTRA, HEAD))

        @pl.when(e > 0)
        def _():
            done[head_at(e), 0:n] = codes
            done[head_at(e), n:n + EXTRA] = extra
            done_copy(e, done, back, send, recv).start()

        @pl.when(e == 0)
        def _():
            back[p, 0:n] = codes
            back[p, n:n + EXTRA] = extra

    def finish_a(e):
        h = head_at(e)
        parts = [part_of(part_a.at[k, h])]
        for d in range(1, K):
            kk = lax.rem(k + d, K)
            remote(
                code_a.at[kk, h], got_a.at[kk, h], part_a_send.at[d, e], got_a_recv.at[kk, h],
                at_k(d),
            ).wait_recv()
            parts.append(sent_part_of(got_a.at[kk, h]))
        finish(e, parts, done_a, back_a, done_a_send, done_a_recv)

    def finish_b(e):
        h = head_at(e)
        parts = [part_of(part_b.at[s, h])]
        for d in range(1, Q):
            qq = lax.rem(q + d, Q)
            remote(
                code_b.at[qq, h], got_b.at[qq, h], part_b_send.at[d, e],
                got_b_recv.at[qq, h], at_q(d),
            ).wait_recv()
            parts.append(sent_part_of(got_b.at[qq, h]))
        finish(e, parts, done_b, back_b, done_b_send, done_b_recv)

    def merge_mate(d):
        qq = lax.rem(q + d, Q)
        mate_b_copy(d).wait_recv()

        @pl.loop(0, HEADS)
        def _(e):
            h = head_at(e)
            both = merged([part_of(part_b.at[qq * 2 + c, h]), part_of(mate_b.at[qq, h])])

            @pl.when(d > 0)
            def _():
                codes, extra = packed_part(*both)
                code_b[qq, h, 0:HEAD] = codes
                code_b[qq, h, HEAD:HEAD + EXTRA] = extra
                part_b_copy(d, e).start()

            @pl.when(d == 0)
            def _():
                part_b[qq * 2 + c, h, 0:HEAD] = both[0]
                part_b[qq * 2 + c, h, HEAD:HEAD + 1] = both[2]
                part_b[qq * 2 + c, h, HEAD + 1:HEAD + 2] = both[1]

    @pl.loop(0, 2 * Q)
    def _(t):
        d = lax.rem(t + 1, Q)
        first = t < Q
        col_block(lax.rem(q + d, Q) * 2 + jnp.where(first, 1 - c, c))

        @pl.when(first)
        def _():
            mate_b_copy(d).start()

        @pl.when(t == 0)
        def _():
            pl.loop(1, HEADS)(lambda e: pass_b(e, 1))
            mate_copy(0, 1).start()

        @pl.when(t == Q)
        def _():
            pass_b_to_mate(1)

        @pl.when(t >= Q)
        def _():
            merge_mate(d)

    for d in range(Q):
        wait_b(lax.rem(q + d, Q) * 2 + 1 - c, 1, mate)

    @pl.loop(0, HEADS + 1)
    def _(n):
        @pl.when(n < HEADS)
        def _():
            e = lax.rem(n + 1, HEADS)
            row_block(e)
            for d in range(1, K):
                part_a_copy(d, e).start()

        @pl.when(n > 0)
        def _():
            finish_b(lax.rem(n, HEADS))
            finish_a(lax.rem(n, HEADS))

    @pl.loop(1, HEADS)
    def _(e):
        for i in range(2):
            cut_b_copy(e, i).wait_send()
            cut_a_copy(e, i).wait_send()

    @pl.loop(0, HEADS)
    def _(e):
        for d in range(1, K):
            for i in range(2):
                a_copy(d, e, i).wait_send()
            part_a_copy(d, e).wait_send()
        for d in range(1, Q):
            for i in range(2):
                b_copy(d, e, i).wait_send()
            part_b_copy(d, e).wait_send()

    for d in range(Q):
        for i in range(2):
            mate_copy(d, i).wait_send()
        mate_b_copy(d).wait_send()

    @pl.loop(1, HEADS)
    def _(e):
        done_copy(e, done_a, back_a, done_a_send, done_a_recv).wait_send()
        done_copy(e, done_b, back_b, done_b_send, done_b_recv).wait_send()
        wait_done(e, done_b, back_b, done_b_send, done_b_recv)
        wait_done(e, done_a, back_a, done_a_send, done_a_recv)


def decode(back_a, back_b, out_a, out_b):
    for back, out in ((back_a, out_a), (back_b, out_b)):
        n = out.shape[0]
        for h in range(HEADS):
            scale = back[h, n:n + EXTRA].astype(jnp.float32)[0:1]
            out[:, h * HEAD:(h + 1) * HEAD] = value_of(back[h, 0:n], scale)


def on_device(rows, cols, rep_a, val_a, rep_b, val_b):
    Q, K = rows // HEADS, cols // 2
    n_a, n_b = rep_a.shape[0], rep_b.shape[0]
    f32, bf16 = jnp.float32, jnp.bfloat16
    tall = HEAD + STATS
    dma = pltpu.SemaphoreType.DMA
    vmem = pl.BlockSpec(memory_space=pltpu.VMEM)
    hbm = pl.BlockSpec(memory_space=pltpu.HBM)
    tile = K * HEADS * n_a * 2 * Q * HEADS * n_b
    back_a, back_b = pl.pallas_call(
        functools.partial(kernel, rows, cols),
        out_shape=(
            jax.ShapeDtypeStruct((HEADS, n_a + EXTRA, HEAD), bf16),
            jax.ShapeDtypeStruct((HEADS, n_b + EXTRA, HEAD), bf16),
        ),
        in_specs=[hbm] * 4,
        out_specs=(vmem, vmem),
        scratch_shapes=[
            pltpu.VMEM((HEADS, K, 2, n_a, HEAD), bf16),
            pltpu.VMEM((2 * Q, HEADS, 2, n_b, HEAD), bf16),
            pltpu.VMEM((HEAD, HEADS * K * n_a), bf16),
            pltpu.VMEM((2 * Q, K * HEADS * n_a, HEADS * n_b), f32),
            pltpu.VMEM((HEADS, K * n_a, HEAD), f32),
            pltpu.VMEM((2 * Q, 8, HEADS * n_b), f32),
            pltpu.VMEM((K, HEADS, tall, n_a), f32),
            pltpu.VMEM((K, HEADS, HEAD + EXTRA, n_a), bf16),
            pltpu.VMEM((K, HEADS, HEAD + EXTRA, n_a), bf16),
            pltpu.VMEM((2 * Q, HEADS, tall, n_b), f32),
            pltpu.VMEM((Q, HEADS, tall, n_b), f32),
            pltpu.VMEM((Q, HEADS, HEAD + EXTRA, n_b), bf16),
            pltpu.VMEM((Q, HEADS, HEAD + EXTRA, n_b), bf16),
            pltpu.VMEM((HEADS, n_a + EXTRA, HEAD), bf16),
            pltpu.VMEM((HEADS, n_b + EXTRA, HEAD), bf16),
            dma((4,)), dma((HEADS, 2)), dma((HEADS, 2)),
            dma((K, HEADS, 2)), dma((2 * Q, HEADS, 2)),
            dma((K, 2)), dma((2 * Q, 2)),
            dma((K, HEADS, 2)), dma((Q, HEADS, 2)), dma((Q, 2)),
            dma((K, HEADS)), dma((K, HEADS)),
            dma((Q,)), dma((Q,)),
            dma((Q, HEADS)), dma((Q, HEADS)),
            dma((HEADS,)), dma((HEADS,)), dma((HEADS,)), dma((HEADS,)),
        ],
        compiler_params=pltpu.CompilerParams(
            collective_id=0, has_side_effects=True, vmem_limit_bytes=GRANT
        ),
        cost_estimate=pl.CostEstimate(
            flops=6 * tile * HEAD, bytes_accessed=6 * 1024 * (n_a + n_b), transcendentals=2 * tile
        ),
    )(rep_a, val_a, rep_b, val_b)
    return pl.pallas_call(
        decode,
        out_shape=(
            jax.ShapeDtypeStruct(rep_a.shape, f32),
            jax.ShapeDtypeStruct(rep_b.shape, f32),
        ),
        in_specs=[vmem] * 2,
        out_specs=(vmem, vmem),
        compiler_params=pltpu.CompilerParams(vmem_limit_bytes=GRANT),
    )(back_a, back_b)


def solution(mesh):
    rows, cols = mesh.shape["row"], mesh.shape["col"]
    placed = P(("row", "col"), None)
    return jax.shard_map(
        functools.partial(on_device, rows, cols),
        mesh=mesh,
        in_specs=(placed,) * 4,
        out_specs=(placed, placed),
        check_vma=False,
    )
```
